256 devices in a mesh: ka: 64 (over z, x, y_hi), band: 4 (over y_lo, core).
Axes of the slice: x: 4, y: 4 (y_hi: 2, y_lo: 2; y = y_hi * 2 + y_lo), z: 8, core: 2. Of those that a mesh axis runs over, the one named last changes fastest.
Arguments:
- occupied: bfloat16 [128, 8, 4096], P('ka'), may hold values from -6 to 6
- virtual: bfloat16 [128, 128, 4096], P('ka', 'band'), may hold values from -6 to 6
- occ_energy: float32 [128, 8], P('ka'), may hold values from -2 to -0.5
- virt_energy: float32 [128, 128], P(None, 'band'), may hold values from 0.5 to 2
- partner: int32 [2, 128], replicated, may hold values from 0 to 127, as said below
- coulomb: float32 [2, 512], replicated, may hold values from 0.5 to 2
- basis: bfloat16 [512, 4096], replicated, may hold values from -0.09375 to 0.09375
Outputs:
- occ_update: bfloat16 [128, 8, 4096], P('ka', None, 'band')
- virt_update: bfloat16 [128, 128, 4096], P('ka', 'band')
The draws below stay inside these ranges and needn't reach their ends.
Inputs may be any that keep to these rules, and one draw needn't show every extreme that they name: Each row pairs the 128 k-points: partner[q, partner[q, k]] == k and partner[q, k] != k.
All inputs are finite; a program needn't handle non-finite values.
Results may differ from the reference program's by a relative error of at most 0.012.
Values may be sent and summed in bfloat16 or wider, within the bound.
A program may use at most 64 MiB of HBM per device.

```python
import math
import jax
import jax.numpy as jnp
from jax import lax

OCC = 8
G = 4096
NAUX = 512
NQ = 2
NK = 128
VIRT = 128


def draw_partner(key, part):
    tables = []
    for transfer in range(NQ):
        order = jax.random.permutation(jax.random.fold_in(key, 101 + transfer), NK).astype(jnp.int32)
        firsts = order[0::2]
        seconds = order[1::2]
        table = jnp.zeros((NK,), jnp.int32).at[firsts].set(seconds).at[seconds].set(firsts)
        tables.append(table)
    return jnp.stack(tables).astype(jnp.int32)


def levels(stream_key, dims, split, smallest, top_value):
    factor_of, own = 1.0, jax.random.fold_in(stream_key, 6)
    for position, blocks in split:
        steps = jnp.exp(jax.random.uniform(jax.random.fold_in(own, position), (blocks,), jnp.float32, smallest / len(split), top_value / len(split)))
        factor_of = factor_of * jnp.repeat(steps, dims[position] // blocks).reshape([-1 if axis == position else 1 for axis in range(len(dims))])
    return factor_of


def scatter_about(rng, extent, spread, bound, split=(), held_as=jnp.bfloat16):
    result = jax.random.normal(rng, extent, jnp.float32) * spread
    if len(split) > 0:
        result = levels(rng, extent, split, -0.22, 0.18) * result
    return jnp.clip(result, min=-bound, max=bound).astype(held_as)


def setup_inputs(seed: int = 0) -> dict:
    keys = jax.random.split(jax.random.key(seed), 8)
    occupied = scatter_about(keys[0], (NK, OCC, G), 1.0, 6.0, ((0, 64),))
    virtual = scatter_about(keys[1], (NK, VIRT, G), 1.0, 6.0, ((0, 64), (1, 4)))
    occ_energy = jnp.clip(-2.0 + 1.5 * jax.random.uniform(keys[2], (NK, OCC), jnp.float32) ** levels(keys[2], (NK, OCC), ((0, 64),), -0.2, 0.2), -2.0, -0.5)
    virt_energy = jnp.clip(0.5 + 1.5 * jax.random.uniform(keys[3], (NK, VIRT), jnp.float32) ** levels(keys[3], (NK, VIRT), ((1, 4),), -0.2, 0.2), 0.5, 2.0)
    partner = draw_partner(jax.random.fold_in(keys[7], 71), 0)
    coulomb = jnp.clip(jnp.exp(jax.random.uniform(keys[5], (NQ, NAUX), jnp.float32, math.log(0.5), math.log(2.0))), 0.5, 2.0)
    basis = scatter_about(keys[6], (NAUX, G), G ** -0.5, 0.09375)
    return {"occupied": occupied, "virtual": virtual, "occ_energy": occ_energy, "virt_energy": virt_energy, "partner": partner, "coulomb": coulomb, "basis": basis}


FREQUENCY = 2.5
BROADENING = 0.4

def response(energy_gaps):
    shifted = FREQUENCY - energy_gaps
    return shifted / (shifted * shifted + BROADENING * BROADENING)

def contract_grid(left, right):
    return lax.dot_general(left, right, (((1,), (1,)), ((), ())), preferred_element_type=jnp.float32)

def contract_rows(left, right):
    return lax.dot_general(left, right, (((0,), (0,)), ((), ())), preferred_element_type=jnp.float32)

def reference(occupied, virtual, occ_energy, virt_energy, partner, coulomb, basis):
    gram_scale = 1.0 / math.sqrt(NK * OCC * VIRT * NAUX)
    occ_scale = 1.0 / math.sqrt(NQ * VIRT)
    occ_total = jnp.zeros((NK, OCC, G), jnp.float32)
    virt_total = jnp.zeros((NK, VIRT, G), jnp.float32)
    for transfer in range(NQ):
        partners = partner[transfer].astype(jnp.int32)
        partner_virt = jnp.take(virtual, partners, axis=0)
        partner_energy = jnp.take(virt_energy, partners, axis=0)
        weights = response(partner_energy[:, None, :] - occ_energy[:, :, None])

        def project(inputs):
            occ_k, virt_k = inputs
            pair_rows = (occ_k[:, None, :] * virt_k[None, :, :]).reshape(OCC * VIRT, G)
            return contract_grid(pair_rows, basis).astype(jnp.bfloat16)
        coeffs = lax.map(project, (occupied, partner_virt))
        flat_coeffs = coeffs.reshape(NK * OCC * VIRT, NAUX)
        weighted = (flat_coeffs.astype(jnp.float32) * weights.reshape(-1, 1)).astype(jnp.bfloat16)
        gram_block = contract_rows(weighted, flat_coeffs)
        screen_block = (coulomb[transfer][:, None] * gram_block * coulomb[transfer][None, :] * gram_scale).astype(jnp.bfloat16)

        def respond(inputs):
            coeff_k, occ_k, virt_k = inputs
            screened = jnp.dot(coeff_k, screen_block, preferred_element_type=jnp.float32).astype(jnp.bfloat16)
            grid_field = jnp.dot(screened, basis, preferred_element_type=jnp.float32).astype(jnp.bfloat16)
            grid_field = grid_field.reshape(OCC, VIRT, G).astype(jnp.float32)
            occ_term = lax.optimization_barrier(jnp.sum(grid_field * virt_k.astype(jnp.float32)[None, :, :], axis=1))
            virt_term = lax.optimization_barrier(jnp.sum(grid_field * occ_k.astype(jnp.float32)[:, None, :], axis=0)).astype(jnp.bfloat16)
            return (occ_term, virt_term)
        occ_term, virt_term = lax.map(respond, (coeffs, occupied, partner_virt))
        occ_total = occ_total + occ_term
        virt_total = virt_total + jnp.take(virt_term, partners, axis=0).astype(jnp.float32)
    return ((occ_total * occ_scale).astype(jnp.bfloat16), virt_total.astype(jnp.bfloat16))
```

```python
import math

import jax
import jax.numpy as jnp
from jax import lax
from jax.sharding import PartitionSpec as P

FREQUENCY = 2.5
BROADENING = 0.4


def response(energy_gaps):
    shifted = FREQUENCY - energy_gaps
    return shifted / (shifted * shifted + BROADENING * BROADENING)


def shards(occupied, virtual, occ_energy, virt_energy, partner, coulomb, basis):
    local_k, occ_count, grid_count = occupied.shape
    group_count = virtual.shape[1]
    aux_count = basis.shape[0]
    transfers = partner.shape[0]
    ka_size = lax.axis_size("ka")
    band_size = lax.axis_size("band")
    total_k = local_k * ka_size
    virt_count = group_count * band_size
    gram_scale = 1.0 / math.sqrt(total_k * occ_count * virt_count * aux_count)
    occ_scale = 1.0 / math.sqrt(transfers * virt_count)
    own_k = lax.axis_index("ka") * local_k + jnp.arange(local_k, dtype=jnp.int32)
    width = occ_count * grid_count // ka_size

    slices = lax.all_to_all(
        occupied.reshape(local_k, ka_size, width), "ka", split_axis=1, concat_axis=0, tiled=True
    ).reshape(total_k, width)
    picked = jnp.stack([jnp.take(slices, partner[q], axis=0) for q in range(transfers)])
    partner_occ = lax.all_to_all(picked, "ka", split_axis=1, concat_axis=2, tiled=True)
    partner_occ = partner_occ.reshape(transfers, local_k, occ_count, grid_count)
    all_energy = lax.all_gather(occ_energy, "ka", axis=0, tiled=True)
    partner_energy = jnp.take(all_energy, jnp.take(partner, own_k, axis=1), axis=0)
    own_energy = jnp.take(virt_energy, own_k, axis=0)
    weights = response(own_energy[None, :, None, :] - partner_energy[:, :, :, None])

    pairs = partner_occ[:, :, :, None, :] * virtual[None, :, None, :, :]
    pairs = pairs.reshape(transfers, -1, grid_count)
    coeffs = jnp.einsum("qmr,pr->qmp", pairs, basis, preferred_element_type=jnp.float32)
    coeffs = coeffs.astype(jnp.bfloat16)
    weighted = (coeffs.astype(jnp.float32) * weights.reshape(transfers, -1, 1)).astype(jnp.bfloat16)
    gram = jnp.einsum("qmp,qms->qps", weighted, coeffs, preferred_element_type=jnp.float32)
    gram = lax.psum(gram, ("ka", "band"))
    screen = (coulomb[:, :, None] * gram * coulomb[:, None, :] * gram_scale).astype(jnp.bfloat16)
    screened = jnp.einsum("qmp,qps->qms", coeffs, screen, preferred_element_type=jnp.float32)
    screened = screened.astype(jnp.bfloat16)
    field = jnp.einsum("qmp,pr->qmr", screened, basis, preferred_element_type=jnp.float32)
    field = field.astype(jnp.bfloat16).astype(jnp.float32)
    field = field.reshape(transfers, local_k, occ_count, group_count, grid_count)
    virt_term = jnp.sum(field * partner_occ[:, :, :, None, :].astype(jnp.float32), axis=2)
    virt_update = jnp.sum(virt_term.astype(jnp.bfloat16).astype(jnp.float32), axis=0)
    virt_update = virt_update.astype(jnp.bfloat16)
    occ_term = jnp.sum(field * virtual[None, :, None, :, :].astype(jnp.float32), axis=3)

    occ_term = lax.psum_scatter(
        occ_term.astype(jnp.bfloat16), "band", scatter_dimension=3, tiled=True
    )
    sent = lax.all_to_all(
        occ_term.reshape(transfers, local_k, ka_size, -1), "ka", split_axis=2, concat_axis=1, tiled=True
    ).reshape(transfers, total_k, -1)
    home = sum(
        jnp.take(sent[q], partner[q], axis=0).astype(jnp.float32) for q in range(transfers)
    )
    home = (home * occ_scale).astype(jnp.bfloat16)
    home = lax.all_to_all(home, "ka", split_axis=0, concat_axis=1, tiled=True)
    return home.reshape(local_k, occ_count, grid_count // band_size), virt_update


def solution(mesh):
    in_specs = (
        P("ka", None, None),
        P("ka", "band", None),
        P("ka", None),
        P(None, "band"),
        P(),
        P(),
        P(),
    )
    out_specs = (P("ka", None, "band"), P("ka", "band", None))
    return jax.shard_map(shards, mesh=mesh, in_specs=in_specs, out_specs=out_specs, check_vma=False)
```

```python
import functools
import math

import jax
import jax.numpy as jnp
from jax import lax
from jax.experimental import pallas as pl
from jax.experimental.pallas import tpu as pltpu
from jax.sharding import PartitionSpec as P

FREQUENCY = 2.5
BROADENING = 0.4
F32 = jnp.float32
BF16 = jnp.bfloat16
MESH = pl.DeviceIdType.MESH
PLANE_KA = 8


def response(energy_gaps):
    shifted = FREQUENCY - energy_gaps
    return shifted / (shifted * shifted + BROADENING * BROADENING)


def dot(left, right):
    return lax.dot_general(left, right, (((1,), (0,)), ((), ())), preferred_element_type=F32)


def dot_t(left, right):
    return lax.dot_general(left, right, (((1,), (1,)), ((), ())), preferred_element_type=F32)


def dot_rows(left, right):
    return lax.dot_general(left, right, (((0,), (0,)), ((), ())), preferred_element_type=F32)


def iota(shape, axis):
    return lax.broadcasted_iota(jnp.int32, shape, axis)


def ones_where(mask):
    return jnp.where(mask, 1.0, 0.0).astype(BF16)


def wait_bytes(ref, sem):
    pltpu.make_async_copy(ref, ref, sem).wait()


def kernel(
    ka_size, band_size, gram_scale, occ_scale,
    occ_ref, virt_hbm, occ_en_ref, virt_en_ref, partner_ref, coul_ref, basis_hbm,
    occ_out, virt_out,
    virt, virt_f, basis, en_s, a1_send, a1_recv, a2_send, a2_recv, occp, occ_f, en_f,
    pick_a, pick_c, fold_a, scale_s, coeffs, acc, weighted, tri_f,
    g1_send, g1_recv, g2_send, g2_recv, g3_recv, screen, screened, field, virt_acc, terms,
    cb_send, cb_recv, c1_send, c1_recv, c2_send, c2_recv,
    load_sem, send_sem, recv_sem,
):
    ka = lax.axis_index("ka")
    band = lax.axis_index("band")
    plane_size = PLANE_KA * band_size
    depth = ka_size // PLANE_KA
    place = lax.rem(ka, PLANE_KA) * band_size + band
    level = ka // PLANE_KA
    quarter = occ_ref.shape[2] // band_size
    chunks = quarter // 128

    load_virt = pltpu.make_async_copy(virt_hbm, virt, load_sem.at[0])
    load_basis = pltpu.make_async_copy(basis_hbm, basis, load_sem.at[1])
    load_virt.start()
    load_basis.start()

    def spread(source, target, index):
        @pl.loop(1, ka_size)
        def _(off):
            to = lax.rem(ka + off, ka_size)
            pltpu.make_async_remote_copy(
                src_ref=source.at[to],
                dst_ref=target.at[ka],
                send_sem=send_sem.at[index],
                recv_sem=recv_sem.at[index],
                device_id=(to, band),
                device_id_type=MESH,
            ).start()

        target[ka] = source[ka]

    en_s[...] = jnp.zeros_like(en_s)
    rest = occ_en_ref[...]
    for part in range(3):
        piece = rest.astype(BF16).astype(F32)
        for k in range(2):
            en_s[2 + 2 * part + k : 3 + 2 * part + k, 0:8] = piece[k : k + 1, :]
        rest = rest - piece
    tiles = []
    for c in range(chunks):
        for k in range(2):
            cols = pl.ds(pl.multiple_of(band * quarter + c * 128, 128), 128)
            tiles.append(occ_ref[k, :, cols].astype(F32))
    own = jnp.concatenate(tiles, axis=0).astype(BF16)
    row, col = iota((512, 128), 0), iota((512, 128), 1)
    s, e = row >> 3, row & 7
    split_a = ones_where((e < 2) & ((s >> 3) == (col & 7)) & ((s & 7) == (col >> 4)) & (((col >> 3) & 1) == e))
    sent = dot(split_a, own).reshape(64, 8, 128) + en_s[...][None]
    a1_send[...] = sent.astype(BF16)
    spread(a1_send, a1_recv, 0)

    part_row = 2 + 2 * lax.rem(ka, 3)
    moved_a = jnp.zeros((512, 512), F32)
    moved_c = jnp.zeros((512, 512), F32)
    to_c = ones_where((e == (col & 1)) & (s == (col >> 1)))
    for q in range(2):
        other = partner_ref[q : q + 1, :]
        base = (other >> 1) * 8 + (other & 1)
        to_data = ones_where((e == 2 * q + (col & 1)) & (s == (col >> 1)))
        to_en = ones_where((e == 4 + 2 * q + (col & 1)) & (s == (col >> 1)))
        moved_a += dot_t(to_data, ones_where(row == base))
        moved_a += dot_t(to_en, ones_where(row == base + part_row))
        moved_c += dot_t(to_c, ones_where(row == base + 2 * q))
    pick_a[...] = moved_a.astype(BF16)
    pick_c[...] = moved_c.astype(BF16)
    r2, c2 = iota((256, 512), 0), iota((256, 512), 1)
    fold_a[...] = ones_where(
        ((c2 & 7) == ((r2 >> 3) & 3)) & ((c2 >> 6) == (r2 & 7)) & (((c2 >> 3) & 7) == (r2 >> 5))
    )

    blocks = [(i, j) for i in range(4) for j in range(i, 4)]
    for q in range(2):
        rows_b, cols_b = [], []
        for i in range(4):
            line = coul_ref[q : q + 1, i * 128 : (i + 1) * 128]
            full = jnp.broadcast_to(line, (128, 128))
            cols_b.append(full)
            rows_b.append(full.T)
        for n, (i, j) in enumerate(blocks):
            scale_s[q, n * 128 : (n + 1) * 128, :] = rows_b[i] * cols_b[j] * gram_scale

    diag = iota((32, 32), 0) == iota((32, 32), 1)
    virt_cols = []
    for k in range(2):
        line = virt_en_ref[pl.ds(2 * ka + k, 1), :]
        full = jnp.where(diag, jnp.broadcast_to(line, (32, 32)), 0.0)
        virt_cols.append(jnp.broadcast_to(jnp.sum(full, axis=1, keepdims=True), (32, 128)))

    load_virt.wait()
    virt_f[...] = virt[...].astype(F32)

    wait_bytes(a1_recv.at[pl.ds(0, ka_size - 1)], recv_sem.at[0])
    got = a1_recv[...].astype(F32).reshape(512, 128).astype(BF16)
    a2_send[...] = dot(pick_a[...], got).reshape(64, 8, 128).astype(BF16)
    spread(a2_send, a2_recv, 1)
    wait_bytes(a2_recv.at[pl.ds(0, ka_size - 1)], recv_sem.at[1])
    got = a2_recv[...].astype(F32).reshape(512, 128).astype(BF16)
    folded = dot(fold_a[...], got)
    for c in range(chunks):
        occp[band, :, c * 128 : (c + 1) * 128] = folded[c * 32 : (c + 1) * 32].astype(BF16)
    en_f[...] = (
        a2_recv[0].astype(F32) + a2_recv[1].astype(F32) + a2_recv[2].astype(F32)
    )
    for off in range(1, band_size):
        to = lax.rem(band + off, band_size)
        pltpu.make_async_remote_copy(
            src_ref=occp.at[band],
            dst_ref=occp.at[band],
            send_sem=send_sem.at[2],
            recv_sem=recv_sem.at[2],
            device_id=(ka, to),
            device_id_type=MESH,
        ).start()
    load_basis.wait()
    wait_bytes(occp.at[pl.ds(0, band_size - 1)], recv_sem.at[2])
    occ_f[...] = occp[...].astype(F32)

    def project(q):
        for b in range(band_size):
            cols = slice(b * quarter, (b + 1) * quarter)
            right = basis[:, cols]
            for k in range(2):
                pieces = []
                for i in range(8):
                    n = (2 * q + k) * 8 + i
                    line = jnp.broadcast_to(occ_f[b, n : n + 1, :], (16, quarter)).astype(BF16)
                    pieces.append(virt[k, 0:16, cols] * line)
                    pieces.append(virt[k, 16:32, cols] * line)
                part = dot_t(jnp.concatenate(pieces, axis=0), right)
                rows = slice(k * 256, (k + 1) * 256)
                if b == 0:
                    acc[rows, :] = part
                else:
                    acc[rows, :] += part
        coeffs[q] = acc[...].astype(BF16)
        for k in range(2):
            for i in range(8):
                n = 4 + 2 * q + k
                energy = jnp.broadcast_to(en_f[n : n + 1, i : i + 1], (32, 128))
                weight = response(virt_cols[k] - energy)
                rows = slice(k * 256 + i * 32, k * 256 + (i + 1) * 32)
                for j in range(4):
                    cols = slice(j * 128, (j + 1) * 128)
                    weighted[rows, cols] = (coeffs[q, rows, cols].astype(F32) * weight).astype(BF16)
        n = 0
        for i in range(4):
            part = dot_rows(weighted[:, i * 128 : (i + 1) * 128], coeffs[q, :, i * 128 :])
            for j in range(4 - i):
                tri_f[n * 128 : (n + 1) * 128, :] = part[:, j * 128 : (j + 1) * 128]
                n += 1

        @pl.loop(0, plane_size)
        def _(c):
            g1_send[q, c] = tri_f[pl.ds(pl.multiple_of(c * 40, 8), 40), :].astype(BF16)

        @pl.loop(1, plane_size)
        def _(off):
            to = lax.rem(place + off, plane_size)
            pltpu.make_async_remote_copy(
                src_ref=g1_send.at[q, to],
                dst_ref=g1_recv.at[q, place],
                send_sem=send_sem.at[3 + q],
                recv_sem=recv_sem.at[3 + q],
                device_id=(level * PLANE_KA + to // band_size, lax.rem(to, band_size)),
                device_id_type=MESH,
            ).start()

        g1_recv[q, place] = g1_send[q, place]

    def exchange(q):
        wait_bytes(g1_recv.at[q, pl.ds(0, plane_size - 1)], recv_sem.at[3 + q])
        total = jnp.sum(g1_recv[q].astype(F32), axis=0).astype(BF16)
        g2_send[q] = total
        g2_recv[q, level] = total

        @pl.loop(1, depth)
        def _(off):
            to = lax.rem(level + off, depth)
            pltpu.make_async_remote_copy(
                src_ref=g2_send.at[q],
                dst_ref=g2_recv.at[q, level],
                send_sem=send_sem.at[5 + q],
                recv_sem=recv_sem.at[5 + q],
                device_id=(to * PLANE_KA + lax.rem(ka, PLANE_KA), band),
                device_id_type=MESH,
            ).start()

    def collect(q):
        wait_bytes(g2_recv.at[q, pl.ds(0, depth - 1)], recv_sem.at[5 + q])
        total = jnp.sum(g2_recv[q].astype(F32), axis=0)
        scale = scale_s[q, pl.ds(pl.multiple_of(place * 40, 8), 40), :]
        g3_recv[q, place] = (total * scale).astype(BF16)

        @pl.loop(1, plane_size)
        def _(off):
            to = lax.rem(place + off, plane_size)
            pltpu.make_async_remote_copy(
                src_ref=g3_recv.at[q, place],
                dst_ref=g3_recv.at[q, place],
                send_sem=send_sem.at[7 + q],
                recv_sem=recv_sem.at[7 + q],
                device_id=(level * PLANE_KA + to // band_size, lax.rem(to, band_size)),
                device_id_type=MESH,
            ).start()

    def respond(q):
        wait_bytes(g3_recv.at[q, pl.ds(0, plane_size - 1)], recv_sem.at[7 + q])

        @pl.loop(0, plane_size)
        def _(c):
            tri_f[pl.ds(pl.multiple_of(c * 40, 8), 40), :] = g3_recv[q, c].astype(F32)

        for n, (i, j) in enumerate(blocks):
            block = tri_f[n * 128 : (n + 1) * 128, :]
            screen[i * 128 : (i + 1) * 128, j * 128 : (j + 1) * 128] = block.astype(BF16)
            if i != j:
                screen[j * 128 : (j + 1) * 128, i * 128 : (i + 1) * 128] = block.T.astype(BF16)
        screened[...] = dot(coeffs[q], screen[...]).astype(BF16)
        width = field.shape[1]
        per = quarter // width
        for b in range(band_size):

            @pl.loop(0, per)
            def _(c):
                cols = pl.ds(pl.multiple_of(b * quarter + c * width, 128), width)
                inner = pl.ds(pl.multiple_of(c * width, 128), width)
                field[...] = dot(screened[...], basis[:, cols])
                for k in range(2):
                    near = virt_f[k, :, cols]
                    total = jnp.zeros((32, width), F32)
                    lines = []
                    for i in range(8):
                        n = (2 * q + k) * 8 + i
                        part = field[k * 256 + i * 32 : k * 256 + (i + 1) * 32, :]
                        total += part * occ_f[b, n : n + 1, inner]
                        lines.append(jnp.sum(part * near, axis=0, keepdims=True))
                    first = (2 * q + k) * 8
                    terms[b, first : first + 8, inner] = jnp.concatenate(lines, axis=0)
                    rounded = total.astype(BF16).astype(F32)
                    if q == 0:
                        virt_acc[k, :, cols] = rounded
                    else:
                        virt_out[k, :, cols] = (virt_acc[k, :, cols] + rounded).astype(BF16)

    project(0)
    project(1)
    exchange(0)
    exchange(1)
    collect(0)
    collect(1)
    respond(0)
    respond(1)

    cb_send[...] = terms[...].astype(BF16)
    for off in range(1, band_size):
        to = lax.rem(band + off, band_size)
        pltpu.make_async_remote_copy(
            src_ref=cb_send.at[to],
            dst_ref=cb_recv.at[band],
            send_sem=send_sem.at[9],
            recv_sem=recv_sem.at[9],
            device_id=(ka, to),
            device_id_type=MESH,
        ).start()
    cb_recv[band] = cb_send[band]
    r2, c2 = iota((512, 256), 0), iota((512, 256), 1)
    split_c = ones_where(
        ((r2 & 7) == ((c2 >> 3) & 3)) & ((r2 >> 6) == (c2 & 7)) & (((r2 >> 3) & 7) == (c2 >> 5))
    )
    r2, c2 = iota((128, 512), 0), iota((128, 512), 1)
    fold_c = ones_where(
        ((c2 & 7) == ((r2 >> 3) & 1)) & ((c2 >> 6) == (r2 & 7)) & (((c2 >> 3) & 7) == (r2 >> 4))
    )
    wait_bytes(cb_recv.at[pl.ds(0, band_size - 1)], recv_sem.at[9])
    total = jnp.sum(cb_recv[...].astype(F32), axis=0)
    tall = jnp.concatenate([total[:, c * 128 : (c + 1) * 128] for c in range(chunks)], axis=0)
    c1_send[...] = dot(split_c, tall.astype(BF16)).reshape(64, 8, 128).astype(BF16)
    spread(c1_send, c1_recv, 10)
    wait_bytes(c1_recv.at[pl.ds(0, ka_size - 1)], recv_sem.at[10])
    got = c1_recv[...].astype(F32).reshape(512, 128).astype(BF16)
    c2_send[...] = (dot(pick_c[...], got) * occ_scale).reshape(64, 8, 128).astype(BF16)
    spread(c2_send, c2_recv, 11)
    wait_bytes(c2_recv.at[pl.ds(0, ka_size - 1)], recv_sem.at[11])
    got = c2_recv[...].astype(F32).reshape(512, 128).astype(BF16)
    folded = dot(fold_c, got)
    for c in range(chunks):
        for k in range(2):
            first = c * 16 + k * 8
            occ_out[k, :, c * 128 : (c + 1) * 128] = folded[first : first + 8].astype(BF16)

    for index, buffer in ((0, a1_recv), (1, a2_recv), (10, c1_recv), (11, c2_recv)):
        wait_bytes(buffer.at[pl.ds(0, ka_size - 1)], send_sem.at[index])
    for index, buffer in ((2, occp), (9, cb_recv)):
        wait_bytes(buffer.at[pl.ds(0, band_size - 1)], send_sem.at[index])
    for q in range(2):
        wait_bytes(g1_recv.at[q, pl.ds(0, plane_size - 1)], send_sem.at[3 + q])
        wait_bytes(g2_recv.at[q, pl.ds(0, depth - 1)], send_sem.at[5 + q])
        wait_bytes(g3_recv.at[q, pl.ds(0, plane_size - 1)], send_sem.at[7 + q])


def shards(occupied, virtual, occ_energy, virt_energy, partner, coulomb, basis):
    local_k, occ_count, grid_count = occupied.shape
    group_count = virtual.shape[1]
    aux_count = basis.shape[0]
    transfers = partner.shape[0]
    ka_size = lax.axis_size("ka")
    band_size = lax.axis_size("band")
    total_k = local_k * ka_size
    virt_count = group_count * band_size
    quarter = grid_count // band_size
    gram_scale = 1.0 / math.sqrt(total_k * occ_count * virt_count * aux_count)
    occ_scale = 1.0 / math.sqrt(transfers * virt_count)
    plane = PLANE_KA * band_size
    depth = ka_size // PLANE_KA
    hop = pltpu.VMEM((ka_size, 8, 128), BF16)
    vmem = pl.BlockSpec(memory_space=pltpu.VMEM)
    hbm = pl.BlockSpec(memory_space=pl.ANY)
    scratch = dict(
        virt=pltpu.VMEM((2, 32, grid_count), BF16),
        virt_f=pltpu.VMEM((2, 32, grid_count), F32),
        basis=pltpu.VMEM((aux_count, grid_count), BF16),
        en_s=pltpu.VMEM((8, 128), F32),
        a1_send=hop,
        a1_recv=hop,
        a2_send=hop,
        a2_recv=hop,
        occp=pltpu.VMEM((band_size, 32, quarter), BF16),
        occ_f=pltpu.VMEM((band_size, 32, quarter), F32),
        en_f=pltpu.VMEM((8, 128), F32),
        pick_a=pltpu.VMEM((512, 512), BF16),
        pick_c=pltpu.VMEM((512, 512), BF16),
        fold_a=pltpu.VMEM((256, 512), BF16),
        scale_s=pltpu.VMEM((2, 1280, 128), F32),
        coeffs=pltpu.VMEM((2, 512, aux_count), BF16),
        acc=pltpu.VMEM((512, aux_count), F32),
        weighted=pltpu.VMEM((512, aux_count), BF16),
        tri_f=pltpu.VMEM((1280, 128), F32),
        g1_send=pltpu.VMEM((2, plane, 40, 128), BF16),
        g1_recv=pltpu.VMEM((2, plane, 40, 128), BF16),
        g2_send=pltpu.VMEM((2, 40, 128), BF16),
        g2_recv=pltpu.VMEM((2, depth, 40, 128), BF16),
        g3_recv=pltpu.VMEM((2, plane, 40, 128), BF16),
        screen=pltpu.VMEM((aux_count, aux_count), BF16),
        screened=pltpu.VMEM((512, aux_count), BF16),
        field=pltpu.VMEM((512, 256), F32),
        virt_acc=pltpu.VMEM((2, 32, grid_count), F32),
        terms=pltpu.VMEM((band_size, 32, quarter), F32),
        cb_send=pltpu.VMEM((band_size, 32, quarter), BF16),
        cb_recv=pltpu.VMEM((band_size, 32, quarter), BF16),
        c1_send=hop,
        c1_recv=hop,
        c2_send=hop,
        c2_recv=hop,
        load_sem=pltpu.SemaphoreType.DMA((2,)),
        send_sem=pltpu.SemaphoreType.DMA((12,)),
        recv_sem=pltpu.SemaphoreType.DMA((12,)),
    )
    return pl.pallas_call(
        functools.partial(kernel, ka_size, band_size, gram_scale, occ_scale),
        out_shape=(
            jax.ShapeDtypeStruct((local_k, occ_count, quarter), BF16),
            jax.ShapeDtypeStruct(virtual.shape, BF16),
        ),
        in_specs=[vmem, hbm, vmem, vmem, vmem, vmem, hbm],
        out_specs=(vmem, vmem),
        scratch_shapes=list(scratch.values()),
        compiler_params=pltpu.CompilerParams(
            has_side_effects=True, vmem_limit_bytes=48 * 1024 * 1024
        ),
    )(occupied, virtual, occ_energy, virt_energy, partner, coulomb, basis)


def solution(mesh):
    in_specs = (
        P("ka", None, None),
        P("ka", "band", None),
        P("ka", None),
        P(None, "band"),
        P(),
        P(),
        P(),
    )
    out_specs = (P("ka", None, "band"), P("ka", "band", None))
    return jax.shard_map(shards, mesh=mesh, in_specs=in_specs, out_specs=out_specs, check_vma=False)
```

```python
import functools
import math

import jax
import jax.numpy as jnp
from jax import lax
from jax.experimental import pallas as pl
from jax.experimental.pallas import tpu as pltpu
from jax.sharding import PartitionSpec as P

FREQUENCY = 2.5
BROADENING = 0.4
F32 = jnp.float32
BF16 = jnp.bfloat16
MESH = pl.DeviceIdType.MESH
PLANE_KA = 8


def response(energy_gaps):
    shifted = FREQUENCY - energy_gaps
    return shifted / (shifted * shifted + BROADENING * BROADENING)


def dot(left, right):
    return lax.dot_general(left, right, (((1,), (0,)), ((), ())), preferred_element_type=F32)


def dot_t(left, right):
    return lax.dot_general(left, right, (((1,), (1,)), ((), ())), preferred_element_type=F32)


def dot_rows(left, right):
    return lax.dot_general(left, right, (((0,), (0,)), ((), ())), preferred_element_type=F32)


def iota(shape, axis):
    return lax.broadcasted_iota(jnp.int32, shape, axis)


def ones_where(mask):
    return jnp.where(mask, 1.0, 0.0).astype(BF16)


def wait_bytes(ref, sem):
    pltpu.make_async_copy(ref, ref, sem).wait()


def kernel(
    ka_size, band_size, gram_scale, occ_scale,
    occ_hbm, virt_hbm, occ_en_hbm, virt_en_hbm, partner_hbm, coul_hbm, basis_hbm,
    occ_out, virt_out,
    occ_ref, virt, occ_en_ref, virt_en_ref, partner_ref, coul_ref, basis, virt_f, en_s, en_all,
    a1_send, a1_recv, a2_send, a2_recv, occ_b, occ_f, pick_a, pick_c, scale_s, coeffs, pairs_a, pairs_b,
    acc, weighted, tri_f, g1_send, g1_recv, g2_send, g2_recv, g3_recv, screen, screened,
    field_a, field_b, virt_acc, cb_send, cb_recv, c1_send, c1_recv, c2_send, c2_recv, table,
    load_sem, send_sem, recv_sem,
):
    ka = lax.axis_index("ka")
    band = lax.axis_index("band")
    plane_size = PLANE_KA * band_size
    depth = ka_size // PLANE_KA
    place = lax.rem(ka, PLANE_KA) * band_size + band
    level = ka // PLANE_KA
    quarter = occ_hbm.shape[2] // band_size
    chunks = quarter // 128

    barrier = pltpu.get_barrier_semaphore()

    @pl.loop(1, ka_size)
    def _(off):
        to = (lax.rem(ka + off, ka_size), band)
        pl.semaphore_signal(barrier, inc=1, device_id=to, device_id_type=MESH)

    for band_off in range(1, band_size):
        near = lax.rem(band + band_off, band_size)

        @pl.loop(0, PLANE_KA)
        def _(off):
            to = (level * PLANE_KA + lax.rem(ka + off, PLANE_KA), near)
            pl.semaphore_signal(barrier, inc=1, device_id=to, device_id_type=MESH)

    loaded = (
        (occ_hbm, occ_ref), (occ_en_hbm, occ_en_ref), (partner_hbm, partner_ref), (coul_hbm, coul_ref),
        (virt_en_hbm, virt_en_ref), (partner_hbm, table), (virt_hbm, virt), (basis_hbm, basis),
    )
    loads = [pltpu.make_async_copy(a, b, load_sem.at[n]) for n, (a, b) in enumerate(loaded)]
    for load in loads:
        load.start()
    load_occ, load_occ_en, load_partner, load_coul, load_virt_en, load_table, load_virt, load_basis = loads

    def spread(source, target, index):
        @pl.loop(1, ka_size)
        def _(off):
            to = lax.rem(ka + off, ka_size)
            pltpu.make_async_remote_copy(
                src_ref=source.at[to],
                dst_ref=target.at[ka],
                send_sem=send_sem.at[index],
                recv_sem=recv_sem.at[index],
                device_id=(to, band),
                device_id_type=MESH,
            ).start()

        target[ka] = source[ka]

    row, col = iota((128, 128), 0), iota((128, 128), 1)
    slice_of, k_of = row >> 1, row & 1
    split_a = ones_where(
        ((slice_of >> 3) == (col & 7)) & ((slice_of & 7) == (col >> 4)) & (((col >> 3) & 1) == k_of)
    )
    load_occ.wait()
    tiles = []
    for c in range(chunks):
        cols = pl.ds(pl.multiple_of(band * quarter + c * 128, 128), 128)
        tiles += [occ_ref[0, :, cols].astype(F32), occ_ref[1, :, cols].astype(F32)]
    tall = jnp.concatenate(tiles, axis=0).astype(BF16)
    a1_send[...] = dot(split_a, tall).reshape(64, 2, 128).astype(BF16)
    load_occ_en.wait()
    en_s[...] = jnp.zeros_like(en_s)
    en_s[:, 0:8] = occ_en_ref[...]
    pl.semaphore_wait(barrier, ka_size - 1 + (band_size - 1) * PLANE_KA)
    spread(a1_send, a1_recv, 0)

    @pl.loop(1, ka_size)
    def _(off):
        pltpu.make_async_remote_copy(
            src_ref=en_s,
            dst_ref=en_all.at[ka],
            send_sem=send_sem.at[2],
            recv_sem=recv_sem.at[2],
            device_id=(lax.rem(ka + off, ka_size), band),
            device_id_type=MESH,
        ).start()

    en_all[ka] = en_s[...]

    load_partner.wait()
    row, col = iota((256, 128), 0), iota((256, 128), 1)
    own_k = 2 * (row >> 2) + (row & 1)
    table_a = jnp.where(((row >> 1) & 1) == 0, partner_ref[0:1, :].astype(F32), partner_ref[1:2, :].astype(F32))
    source = jnp.sum(jnp.where(col == own_k, table_a, 0.0), axis=1, keepdims=True)
    pick_a[...] = ones_where(col == source.astype(jnp.int32))
    row, col = iota((128, 128), 0), iota((128, 128), 1)
    wide_col = iota((128, 256), 1)
    moved_c = jnp.zeros((128, 256), F32)
    for q in range(2):
        chosen = jnp.where(row == col, partner_ref[q : q + 1, :].astype(F32), 0.0)
        source = jnp.sum(chosen, axis=1, keepdims=True).astype(jnp.int32)
        moved_c += jnp.where(wide_col == (source >> 1) * 4 + 2 * q + (source & 1), 1.0, 0.0)
    pick_c[...] = moved_c.astype(BF16)
    row, col = iota((256, 256), 0), iota((256, 256), 1)
    fold_a = ones_where(
        ((col & 3) == ((row >> 3) & 3)) & ((col >> 5) == (row & 7)) & (((col >> 2) & 7) == (row >> 5))
    )

    load_coul.wait()
    blocks = [(i, j) for i in range(4) for j in range(i, 4)]
    for q in range(2):
        rows_b, cols_b = [], []
        for i in range(4):
            line = coul_ref[q : q + 1, i * 128 : (i + 1) * 128]
            full = jnp.broadcast_to(line, (128, 128))
            cols_b.append(full)
            rows_b.append(full.T)
        for n, (i, j) in enumerate(blocks):
            scale_s[q, n * 128 : (n + 1) * 128, :] = rows_b[i] * cols_b[j] * gram_scale

    load_virt_en.wait()
    virt_cols = []
    for k in range(2):
        full = jnp.where(iota((32, 128), 1) == 2 * ka + k, virt_en_ref[...], 0.0)
        virt_cols.append(jnp.broadcast_to(jnp.sum(full, axis=1, keepdims=True), (32, 128)))

    load_virt.wait()
    virt_f[...] = virt[...].astype(F32)

    wait_bytes(a1_recv.at[pl.ds(0, ka_size - 1)], recv_sem.at[0])
    got = a1_recv[...].astype(F32).reshape(128, 128).astype(BF16)
    a2_send[...] = dot(pick_a[...], got).reshape(64, 4, 128).astype(BF16)
    spread(a2_send, a2_recv, 1)
    load_basis.wait()
    load_table.wait()
    wait_bytes(en_all.at[pl.ds(0, ka_size - 1)], recv_sem.at[2])
    energies = []
    for q in range(2):
        for k in range(2):
            other = table[q, 2 * ka + k]
            energies.append(en_all[other // 2, pl.ds(lax.rem(other, 2), 1), :])
    wait_bytes(a2_recv.at[pl.ds(0, ka_size - 1)], recv_sem.at[1])
    got = a2_recv[...].astype(F32).reshape(256, 128).astype(BF16)
    folded = dot(fold_a, got)
    for q in range(2):
        for c in range(chunks):
            tile = folded[c * 32 + q * 16 : c * 32 + (q + 1) * 16]
            cols = slice(c * 128, (c + 1) * 128)
            occ_b[q, band, :, cols] = tile.astype(BF16)
            occ_f[q, band, :, cols] = tile

    for q in range(2):
        for off in range(1, band_size):
            to = lax.rem(band + band_size - off, band_size)
            pltpu.make_async_remote_copy(
                src_ref=occ_b.at[q, band],
                dst_ref=occ_b.at[q, band],
                send_sem=send_sem.at[13 + q],
                recv_sem=recv_sem.at[13 + 3 * q + off - 1],
                device_id=(ka, to),
                device_id_type=MESH,
            ).start()

    def build(q, b, pairs):
        part = lax.rem(band + b, band_size)
        if b > 0:
            wait_bytes(occ_b.at[q, part], recv_sem.at[13 + 3 * q + b - 1])
            occ_f[q, part] = occ_b[q, part].astype(F32)
        cols = pl.ds(pl.multiple_of(part * quarter, 128), quarter)
        for k in range(2):
            for i in range(8):
                n = k * 8 + i
                line = jnp.broadcast_to(occ_f[q, part, n : n + 1, :], (16, quarter)).astype(BF16)
                first = k * 256 + i * 32
                pairs[first : first + 16, :] = virt[k, 0:16, cols] * line
                pairs[first + 16 : first + 32, :] = virt[k, 16:32, cols] * line
        return cols

    def project(q):
        buffers = (pairs_a, pairs_b)
        cols = build(q, 0, buffers[0])
        for b in range(band_size):
            now = cols
            if b + 1 < band_size:
                cols = build(q, b + 1, buffers[(b + 1) % 2])
            part = dot_t(buffers[b % 2][...], basis[:, now])
            if b == 0:
                acc[...] = part
            else:
                acc[...] += part
        coeffs[q] = acc[...].astype(BF16)
        for k in range(2):
            for i in range(8):
                energy = jnp.broadcast_to(energies[2 * q + k][:, i : i + 1], (32, 128))
                weight = response(virt_cols[k] - energy)
                rows = slice(k * 256 + i * 32, k * 256 + (i + 1) * 32)
                for j in range(4):
                    cols = slice(j * 128, (j + 1) * 128)
                    weighted[rows, cols] = (coeffs[q, rows, cols].astype(F32) * weight).astype(BF16)
        n = 0
        for i in range(4):
            part = dot_rows(weighted[:, i * 128 : (i + 1) * 128], coeffs[q, :, i * 128 :])
            for j in range(4 - i):
                tri_f[n * 128 : (n + 1) * 128, :] = part[:, j * 128 : (j + 1) * 128]
                n += 1

        @pl.loop(0, plane_size)
        def _(c):
            g1_send[q, c] = tri_f[pl.ds(pl.multiple_of(c * 40, 8), 40), :].astype(BF16)

        @pl.loop(1, plane_size)
        def _(off):
            to = lax.rem(place + off, plane_size)
            pltpu.make_async_remote_copy(
                src_ref=g1_send.at[q, to],
                dst_ref=g1_recv.at[q, place],
                send_sem=send_sem.at[3 + q],
                recv_sem=recv_sem.at[3 + q],
                device_id=(level * PLANE_KA + to // band_size, lax.rem(to, band_size)),
                device_id_type=MESH,
            ).start()

        g1_recv[q, place] = g1_send[q, place]

    def exchange(q):
        wait_bytes(g1_recv.at[q, pl.ds(0, plane_size - 1)], recv_sem.at[3 + q])
        total = jnp.sum(g1_recv[q].astype(F32), axis=0).astype(BF16)
        g2_send[q] = total
        g2_recv[q, level] = total

        @pl.loop(1, depth)
        def _(off):
            to = lax.rem(level + off, depth)
            pltpu.make_async_remote_copy(
                src_ref=g2_send.at[q],
                dst_ref=g2_recv.at[q, level],
                send_sem=send_sem.at[5 + q],
                recv_sem=recv_sem.at[5 + q],
                device_id=(to * PLANE_KA + lax.rem(ka, PLANE_KA), band),
                device_id_type=MESH,
            ).start()

    def collect(q):
        wait_bytes(g2_recv.at[q, pl.ds(0, depth - 1)], recv_sem.at[5 + q])
        total = jnp.sum(g2_recv[q].astype(F32), axis=0)
        scale = scale_s[q, pl.ds(pl.multiple_of(place * 40, 8), 40), :]
        g3_recv[q, place] = (total * scale).astype(BF16)

        @pl.loop(1, plane_size)
        def _(off):
            to = lax.rem(place + off, plane_size)
            pltpu.make_async_remote_copy(
                src_ref=g3_recv.at[q, place],
                dst_ref=g3_recv.at[q, place],
                send_sem=send_sem.at[7 + q],
                recv_sem=recv_sem.at[7 + q],
                device_id=(level * PLANE_KA + to // band_size, lax.rem(to, band_size)),
                device_id_type=MESH,
            ).start()

    def prepare(q):
        wait_bytes(g3_recv.at[q, pl.ds(0, plane_size - 1)], recv_sem.at[7 + q])

        @pl.loop(0, plane_size)
        def _(c):
            tri_f[pl.ds(pl.multiple_of(c * 40, 8), 40), :] = g3_recv[q, c].astype(F32)

        for n, (i, j) in enumerate(blocks):
            block = tri_f[n * 128 : (n + 1) * 128, :]
            screen[i * 128 : (i + 1) * 128, j * 128 : (j + 1) * 128] = block.astype(BF16)
            if i != j:
                screen[j * 128 : (j + 1) * 128, i * 128 : (i + 1) * 128] = block.T.astype(BF16)
        screened[...] = dot(coeffs[q], screen[...]).astype(BF16)

    def respond(q):
        step = field_a.shape[1]
        per = quarter // step

        def locate(n):
            part = lax.rem(band + 1 + n // per, band_size)
            inner = pl.multiple_of(lax.rem(n, per) * step, 128)
            cols = pl.ds(pl.multiple_of(part * quarter + inner, 128), step)
            return part, pl.ds(inner, step), cols

        def expand(n, field):
            field[...] = dot(screened[...], basis[:, locate(n)[2]])

        def contract(n, field):
            part, inner, cols = locate(n)
            for k in range(2):
                near = virt_f[k, :, cols]
                total = jnp.zeros((32, step), F32)
                lines = []
                for i in range(8):
                    first = k * 256 + i * 32
                    piece = field[first : first + 32, :]
                    total += piece * occ_f[q, part, k * 8 + i : k * 8 + i + 1, inner]
                    lines.append(jnp.sum(piece * near, axis=0, keepdims=True))
                lines = jnp.concatenate(lines, axis=0)
                cb_send[q, part, k * 8 : (k + 1) * 8, inner] = lines.astype(BF16)
                rounded = total.astype(BF16).astype(F32)
                if q == 0:
                    virt_acc[k, :, cols] = rounded
                else:
                    virt_out[k, :, cols] = (virt_acc[k, :, cols] + rounded).astype(BF16)

        expand(0, field_a)
        for j in range(band_size):

            @pl.loop(0, per // 2)
            def _(t):
                n = j * per + 2 * t
                expand(n + 1, field_b)
                contract(n, field_a)
                expand(lax.rem(n + 2, per * band_size), field_a)
                contract(n + 1, field_b)

            to = lax.rem(band + 1 + j, band_size)
            if j < band_size - 1:
                pltpu.make_async_remote_copy(
                    src_ref=cb_send.at[q, to],
                    dst_ref=cb_recv.at[q, band],
                    send_sem=send_sem.at[9 + 3 * q],
                    recv_sem=recv_sem.at[9 + 3 * q],
                    device_id=(ka, to),
                    device_id_type=MESH,
                ).start()
            else:
                cb_recv[q, band] = cb_send[q, band]

    project(0)
    project(1)
    exchange(0)
    exchange(1)
    collect(0)
    collect(1)
    prepare(0)
    respond(0)
    prepare(1)
    respond(1)

    row, col = iota((256, 128), 0), iota((256, 128), 1)
    sent = jnp.zeros((256, 128), F32)
    for q in range(2):
        split_c = ones_where(
            ((row & 3) == 2 * q + ((col >> 3) & 1)) & ((row >> 5) == (col & 7)) & (((row >> 2) & 7) == (col >> 4))
        )
        wait_bytes(cb_recv.at[q, pl.ds(0, band_size - 1)], recv_sem.at[9 + 3 * q])
        total = jnp.sum(cb_recv[q].astype(F32), axis=0)
        tall = jnp.concatenate([total[:, c * 128 : (c + 1) * 128] for c in range(chunks)], axis=0)
        sent += dot(split_c, tall.astype(BF16))
    c1_send[...] = sent.reshape(64, 4, 128).astype(BF16)
    row, col = iota((128, 128), 0), iota((128, 128), 1)
    fold_c = ones_where(
        ((col & 1) == ((row >> 3) & 1)) & ((col >> 4) == (row & 7)) & (((col >> 1) & 7) == (row >> 4))
    )
    spread(c1_send, c1_recv, 10)
    wait_bytes(c1_recv.at[pl.ds(0, ka_size - 1)], recv_sem.at[10])
    got = c1_recv[...].astype(F32).reshape(256, 128).astype(BF16)
    c2_send[...] = (dot(pick_c[...], got) * occ_scale).reshape(64, 2, 128).astype(BF16)
    spread(c2_send, c2_recv, 11)
    wait_bytes(c2_recv.at[pl.ds(0, ka_size - 1)], recv_sem.at[11])
    got = c2_recv[...].astype(F32).reshape(128, 128).astype(BF16)
    folded = dot(fold_c, got)
    for c in range(chunks):
        for k in range(2):
            first = c * 16 + k * 8
            occ_out[k, :, c * 128 : (c + 1) * 128] = folded[first : first + 8].astype(BF16)

    for index, buffer in ((0, a1_recv), (1, a2_recv), (10, c1_recv), (11, c2_recv)):
        wait_bytes(buffer.at[pl.ds(0, ka_size - 1)], send_sem.at[index])
    wait_bytes(en_all.at[pl.ds(0, ka_size - 1)], send_sem.at[2])
    for q in range(2):
        wait_bytes(cb_recv.at[q, pl.ds(0, band_size - 1)], send_sem.at[9 + 3 * q])
        wait_bytes(occ_b.at[q, pl.ds(0, band_size - 1)], send_sem.at[13 + q])
        wait_bytes(g1_recv.at[q, pl.ds(0, plane_size - 1)], send_sem.at[3 + q])
        wait_bytes(g2_recv.at[q, pl.ds(0, depth - 1)], send_sem.at[5 + q])
        wait_bytes(g3_recv.at[q, pl.ds(0, plane_size - 1)], send_sem.at[7 + q])


def shards(occupied, virtual, occ_energy, virt_energy, partner, coulomb, basis):
    local_k, occ_count, grid_count = occupied.shape
    group_count = virtual.shape[1]
    aux_count = basis.shape[0]
    transfers = partner.shape[0]
    ka_size = lax.axis_size("ka")
    band_size = lax.axis_size("band")
    total_k = local_k * ka_size
    virt_count = group_count * band_size
    quarter = grid_count // band_size
    gram_scale = 1.0 / math.sqrt(total_k * occ_count * virt_count * aux_count)
    occ_scale = 1.0 / math.sqrt(transfers * virt_count)
    plane = PLANE_KA * band_size
    depth = ka_size // PLANE_KA
    hop_2 = pltpu.VMEM((ka_size, 2, 128), BF16)
    hop_4 = pltpu.VMEM((ka_size, 4, 128), BF16)
    virt_energy = virt_energy.T
    vmem = pl.BlockSpec(memory_space=pltpu.VMEM)
    hbm = pl.BlockSpec(memory_space=pl.ANY)
    scratch = dict(
        occ=pltpu.VMEM(occupied.shape, BF16),
        virt=pltpu.VMEM(virtual.shape, BF16),
        occ_en=pltpu.VMEM(occ_energy.shape, F32),
        virt_en=pltpu.VMEM(virt_energy.shape, F32),
        partner=pltpu.VMEM(partner.shape, jnp.int32),
        coul=pltpu.VMEM(coulomb.shape, F32),
        basis=pltpu.VMEM(basis.shape, BF16),
        virt_f=pltpu.VMEM(virtual.shape, F32),
        en_s=pltpu.VMEM((2, 128), F32),
        en_all=pltpu.VMEM((ka_size, 2, 128), F32),
        a1_send=hop_2,
        a1_recv=hop_2,
        a2_send=hop_4,
        a2_recv=hop_4,
        occ_b=pltpu.VMEM((2, band_size, 16, quarter), BF16),
        occ_f=pltpu.VMEM((2, band_size, 16, quarter), F32),
        pick_a=pltpu.VMEM((256, 128), BF16),
        pick_c=pltpu.VMEM((128, 256), BF16),
        scale_s=pltpu.VMEM((2, 1280, 128), F32),
        coeffs=pltpu.VMEM((2, 512, aux_count), BF16),
        pairs_a=pltpu.VMEM((512, quarter), BF16),
        pairs_b=pltpu.VMEM((512, quarter), BF16),
        acc=pltpu.VMEM((512, aux_count), F32),
        weighted=pltpu.VMEM((512, aux_count), BF16),
        tri_f=pltpu.VMEM((1280, 128), F32),
        g1_send=pltpu.VMEM((2, plane, 40, 128), BF16),
        g1_recv=pltpu.VMEM((2, plane, 40, 128), BF16),
        g2_send=pltpu.VMEM((2, 40, 128), BF16),
        g2_recv=pltpu.VMEM((2, depth, 40, 128), BF16),
        g3_recv=pltpu.VMEM((2, plane, 40, 128), BF16),
        screen=pltpu.VMEM((aux_count, aux_count), BF16),
        screened=pltpu.VMEM((512, aux_count), BF16),
        field_a=pltpu.VMEM((512, 256), F32),
        field_b=pltpu.VMEM((512, 256), F32),
        virt_acc=pltpu.VMEM(virtual.shape, F32),
        cb_send=pltpu.VMEM((2, band_size, 16, quarter), BF16),
        cb_recv=pltpu.VMEM((2, band_size, 16, quarter), BF16),
        c1_send=hop_4,
        c1_recv=hop_4,
        c2_send=hop_2,
        c2_recv=hop_2,
        table=pltpu.SMEM(partner.shape, jnp.int32),
        load_sem=pltpu.SemaphoreType.DMA((8,)),
        send_sem=pltpu.SemaphoreType.DMA((15,)),
        recv_sem=pltpu.SemaphoreType.DMA((19,)),
    )
    return pl.pallas_call(
        functools.partial(kernel, ka_size, band_size, gram_scale, occ_scale),
        out_shape=(
            jax.ShapeDtypeStruct((local_k, occ_count, quarter), BF16),
            jax.ShapeDtypeStruct(virtual.shape, BF16),
        ),
        in_specs=[hbm] * 7,
        out_specs=(vmem, vmem),
        scratch_shapes=list(scratch.values()),
        compiler_params=pltpu.CompilerParams(
            collective_id=0, has_side_effects=True, vmem_limit_bytes=60 * 1024 * 1024
        ),
    )(occupied, virtual, occ_energy, virt_energy, partner, coulomb, basis)


def solution(mesh):
    in_specs = (
        P("ka", None, None),
        P("ka", "band", None),
        P("ka", None),
        P(None, "band"),
        P(),
        P(),
        P(),
    )
    out_specs = (P("ka", None, "band"), P("ka", "band", None))
    return jax.shard_map(shards, mesh=mesh, in_specs=in_specs, out_specs=out_specs, check_vma=False)
```

```python
import functools
import math

import jax
import jax.numpy as jnp
from jax import lax
from jax.experimental import pallas as pl
from jax.experimental.pallas import tpu as pltpu
from jax.sharding import PartitionSpec as P

FREQUENCY = 2.5
BROADENING = 0.4
F32 = jnp.float32
BF16 = jnp.bfloat16
MESH = pl.DeviceIdType.MESH
PLANE_KA = 8


def response(energy_gaps):
    shifted = FREQUENCY - energy_gaps
    return shifted / (shifted * shifted + BROADENING * BROADENING)


def dot(left, right):
    return lax.dot_general(left, right, (((1,), (0,)), ((), ())), preferred_element_type=F32)


def dot_t(left, right):
    return lax.dot_general(left, right, (((1,), (1,)), ((), ())), preferred_element_type=F32)


def dot_rows(left, right):
    return lax.dot_general(left, right, (((0,), (0,)), ((), ())), preferred_element_type=F32)


def iota(shape, axis):
    return lax.broadcasted_iota(jnp.int32, shape, axis)


def ones_where(mask):
    return jnp.where(mask, 1.0, 0.0).astype(BF16)


def wait_bytes(ref, sem):
    pltpu.make_async_copy(ref, ref, sem).wait()


def kernel(
    ka_size, band_size, gram_scale, occ_scale,
    occ_hbm, virt_hbm, occ_en_hbm, virt_en_hbm, partner_hbm, coul_hbm, basis_hbm,
    occ_out, virt_out,
    occ_ref, virt, occ_en_ref, virt_en_ref, partner_ref, coul_ref, basis, virt_f, en_s, en_all,
    a1_send, a1_recv, a2_send, a2_recv, occ_b, occ_f, pick_a, pick_c, scale_s, coeffs, pairs_a, pairs_b,
    acc, weighted, tri_f, g1_send, g1_recv, g2_send, g2_recv, g3_recv, screen, screened,
    field_a, field_b, virt_acc, cb_send, cb_recv, c1_send, c1_recv, c2_send, c2_recv, table,
    load_sem, send_sem, recv_sem,
):
    ka = lax.axis_index("ka")
    band = lax.axis_index("band")
    plane_size = PLANE_KA * band_size
    depth = ka_size // PLANE_KA
    place = lax.rem(ka, PLANE_KA) * band_size + band
    level = ka // PLANE_KA
    quarter = occ_hbm.shape[2] // band_size
    chunks = quarter // 128

    barrier = pltpu.get_barrier_semaphore()

    @pl.loop(1, ka_size)
    def _(off):
        to = (lax.rem(ka + off, ka_size), band)
        pl.semaphore_signal(barrier, inc=1, device_id=to, device_id_type=MESH)

    for band_off in range(1, band_size):
        near = lax.rem(band + band_off, band_size)

        @pl.loop(0, PLANE_KA)
        def _(off):
            to = (level * PLANE_KA + lax.rem(ka + off, PLANE_KA), near)
            pl.semaphore_signal(barrier, inc=1, device_id=to, device_id_type=MESH)

    loaded = (
        (occ_hbm, occ_ref), (occ_en_hbm, occ_en_ref), (partner_hbm, partner_ref), (coul_hbm, coul_ref),
        (virt_en_hbm, virt_en_ref), (partner_hbm, table), (virt_hbm, virt), (basis_hbm, basis),
    )
    loads = [pltpu.make_async_copy(a, b, load_sem.at[n]) for n, (a, b) in enumerate(loaded)]
    for load in loads:
        load.start()
    load_occ, load_occ_en, load_partner, load_coul, load_virt_en, load_table, load_virt, load_basis = loads

    def spread(source, target, index):
        @pl.loop(1, ka_size)
        def _(off):
            to = lax.rem(ka + off, ka_size)
            pltpu.make_async_remote_copy(
                src_ref=source.at[to],
                dst_ref=target.at[ka],
                send_sem=send_sem.at[index],
                recv_sem=recv_sem.at[index],
                device_id=(to, band),
                device_id_type=MESH,
            ).start()

        target[ka] = source[ka]

    row, col = iota((128, 128), 0), iota((128, 128), 1)
    slice_of, k_of = row >> 1, row & 1
    split_a = ones_where(
        ((slice_of >> 3) == (col & 7)) & ((slice_of & 7) == (col >> 4)) & (((col >> 3) & 1) == k_of)
    )
    load_occ.wait()
    tiles = []
    for c in range(chunks):
        cols = pl.ds(pl.multiple_of(band * quarter + c * 128, 128), 128)
        tiles += [occ_ref[0, :, cols].astype(F32), occ_ref[1, :, cols].astype(F32)]
    tall = jnp.concatenate(tiles, axis=0).astype(BF16)
    a1_send[...] = dot(split_a, tall).reshape(64, 2, 128).astype(BF16)
    load_occ_en.wait()
    en_s[...] = jnp.zeros_like(en_s)
    en_s[:, 0:8] = occ_en_ref[...]
    pl.semaphore_wait(barrier, ka_size - 1 + (band_size - 1) * PLANE_KA)
    spread(a1_send, a1_recv, 0)

    @pl.loop(1, ka_size)
    def _(off):
        pltpu.make_async_remote_copy(
            src_ref=en_s,
            dst_ref=en_all.at[ka],
            send_sem=send_sem.at[2],
            recv_sem=recv_sem.at[2],
            device_id=(lax.rem(ka + off, ka_size), band),
            device_id_type=MESH,
        ).start()

    en_all[ka] = en_s[...]

    load_partner.wait()
    row, col = iota((256, 128), 0), iota((256, 128), 1)
    own_k = 2 * (row >> 2) + (row & 1)
    table_a = jnp.where(((row >> 1) & 1) == 0, partner_ref[0:1, :].astype(F32), partner_ref[1:2, :].astype(F32))
    source = jnp.sum(jnp.where(col == own_k, table_a, 0.0), axis=1, keepdims=True)
    pick_a[...] = ones_where(col == source.astype(jnp.int32))
    row, col = iota((128, 128), 0), iota((128, 128), 1)
    wide_col = iota((128, 256), 1)
    moved_c = jnp.zeros((128, 256), F32)
    for q in range(2):
        chosen = jnp.where(row == col, partner_ref[q : q + 1, :].astype(F32), 0.0)
        source = jnp.sum(chosen, axis=1, keepdims=True).astype(jnp.int32)
        moved_c += jnp.where(wide_col == (source >> 1) * 4 + 2 * q + (source & 1), 1.0, 0.0)
    pick_c[...] = moved_c.astype(BF16)
    row, col = iota((256, 256), 0), iota((256, 256), 1)
    fold_a = ones_where(
        ((col & 3) == ((row >> 3) & 3)) & ((col >> 5) == (row & 7)) & (((col >> 2) & 7) == (row >> 5))
    )

    load_coul.wait()
    blocks = [(i, j) for i in range(4) for j in range(i, 4)]
    for q in range(2):
        rows_b, cols_b = [], []
        for i in range(4):
            line = coul_ref[q : q + 1, i * 128 : (i + 1) * 128]
            full = jnp.broadcast_to(line, (128, 128))
            cols_b.append(full)
            rows_b.append(full.T)
        for n, (i, j) in enumerate(blocks):
            scale_s[q, n * 128 : (n + 1) * 128, :] = rows_b[i] * cols_b[j] * gram_scale

    load_virt_en.wait()
    virt_cols = []
    for k in range(2):
        full = jnp.where(iota((32, 128), 1) == 2 * ka + k, virt_en_ref[...], 0.0)
        virt_cols.append(jnp.broadcast_to(jnp.sum(full, axis=1, keepdims=True), (32, 128)))

    load_virt.wait()
    virt_f[...] = virt[...].astype(F32)

    wait_bytes(a1_recv.at[pl.ds(0, ka_size - 1)], recv_sem.at[0])
    got = a1_recv[...].astype(F32).reshape(128, 128).astype(BF16)
    a2_send[...] = dot(pick_a[...], got).reshape(64, 4, 128).astype(BF16)
    spread(a2_send, a2_recv, 1)
    load_basis.wait()
    load_table.wait()
    wait_bytes(en_all.at[pl.ds(0, ka_size - 1)], recv_sem.at[2])
    energies = []
    for q in range(2):
        for k in range(2):
            other = table[q, 2 * ka + k]
            energies.append(en_all[other // 2, pl.ds(lax.rem(other, 2), 1), :])
    wait_bytes(a2_recv.at[pl.ds(0, ka_size - 1)], recv_sem.at[1])
    got = a2_recv[...].astype(F32).reshape(256, 128).astype(BF16)
    folded = dot(fold_a, got)
    for q in range(2):
        for c in range(chunks):
            tile = folded[c * 32 + q * 16 : c * 32 + (q + 1) * 16]
            cols = slice(c * 128, (c + 1) * 128)
            occ_b[q, band, :, cols] = tile.astype(BF16)
            occ_f[q, band, :, cols] = tile

    for q in range(2):
        for off in range(1, band_size):
            to = lax.rem(band + band_size - off, band_size)
            pltpu.make_async_remote_copy(
                src_ref=occ_b.at[q, band],
                dst_ref=occ_b.at[q, band],
                send_sem=send_sem.at[13 + q],
                recv_sem=recv_sem.at[13 + 3 * q + off - 1],
                device_id=(ka, to),
                device_id_type=MESH,
            ).start()

    def build(q, b, pairs):
        part = lax.rem(band + b, band_size)
        cols = pl.ds(pl.multiple_of(part * quarter, 128), quarter)
        for k in range(2):
            for i in range(8):
                n = k * 8 + i
                line = jnp.broadcast_to(occ_f[q, part, n : n + 1, :], (16, quarter)).astype(BF16)
                first = k * 256 + i * 32
                pairs[first : first + 16, :] = virt[k, 0:16, cols] * line
                pairs[first + 16 : first + 32, :] = virt[k, 16:32, cols] * line
        return cols

    def begin():
        cols = build(0, 0, pairs_a)
        build(1, 0, pairs_b)
        acc[0] = dot_t(pairs_a[...], basis[:, cols])
        acc[1] = dot_t(pairs_b[...], basis[:, cols])

    def project(q):
        for b in range(1, band_size):
            part = lax.rem(band + b, band_size)
            wait_bytes(occ_b.at[q, part], recv_sem.at[13 + 3 * q + b - 1])
            occ_f[q, part] = occ_b[q, part].astype(F32)
        buffers = (pairs_a, pairs_b)
        cols = build(q, 1, buffers[1])
        for b in range(1, band_size):
            now = cols
            if b + 1 < band_size:
                cols = build(q, b + 1, buffers[(b + 1) % 2])
            acc[q] += dot_t(buffers[b % 2][...], basis[:, now])
        coeffs[q] = acc[q].astype(BF16)
        for k in range(2):
            for i in range(8):
                energy = jnp.broadcast_to(energies[2 * q + k][:, i : i + 1], (32, 128))
                weight = response(virt_cols[k] - energy)
                rows = slice(k * 256 + i * 32, k * 256 + (i + 1) * 32)
                for j in range(4):
                    cols = slice(j * 128, (j + 1) * 128)
                    weighted[rows, cols] = (coeffs[q, rows, cols].astype(F32) * weight).astype(BF16)
        n = 0
        for i in range(4):
            part = dot_rows(weighted[:, i * 128 : (i + 1) * 128], coeffs[q, :, i * 128 :])
            for j in range(4 - i):
                tri_f[n * 128 : (n + 1) * 128, :] = part[:, j * 128 : (j + 1) * 128]
                n += 1

        @pl.loop(0, plane_size)
        def _(c):
            g1_send[q, c] = tri_f[pl.ds(pl.multiple_of(c * 40, 8), 40), :].astype(BF16)

        @pl.loop(1, plane_size)
        def _(off):
            to = lax.rem(place + off, plane_size)
            pltpu.make_async_remote_copy(
                src_ref=g1_send.at[q, to],
                dst_ref=g1_recv.at[q, place],
                send_sem=send_sem.at[3 + q],
                recv_sem=recv_sem.at[3 + q],
                device_id=(level * PLANE_KA + to // band_size, lax.rem(to, band_size)),
                device_id_type=MESH,
            ).start()

        g1_recv[q, place] = g1_send[q, place]

    def exchange(q):
        wait_bytes(g1_recv.at[q, pl.ds(0, plane_size - 1)], recv_sem.at[3 + q])
        total = jnp.sum(g1_recv[q].astype(F32), axis=0).astype(BF16)
        g2_send[q] = total
        g2_recv[q, level] = total

        @pl.loop(1, depth)
        def _(off):
            to = lax.rem(level + off, depth)
            pltpu.make_async_remote_copy(
                src_ref=g2_send.at[q],
                dst_ref=g2_recv.at[q, level],
                send_sem=send_sem.at[5 + q],
                recv_sem=recv_sem.at[5 + q],
                device_id=(to * PLANE_KA + lax.rem(ka, PLANE_KA), band),
                device_id_type=MESH,
            ).start()

    def collect(q):
        wait_bytes(g2_recv.at[q, pl.ds(0, depth - 1)], recv_sem.at[5 + q])
        total = jnp.sum(g2_recv[q].astype(F32), axis=0)
        scale = scale_s[q, pl.ds(pl.multiple_of(place * 40, 8), 40), :]
        g3_recv[q, place] = (total * scale).astype(BF16)

        @pl.loop(1, plane_size)
        def _(off):
            to = lax.rem(place + off, plane_size)
            pltpu.make_async_remote_copy(
                src_ref=g3_recv.at[q, place],
                dst_ref=g3_recv.at[q, place],
                send_sem=send_sem.at[7 + q],
                recv_sem=recv_sem.at[7 + q],
                device_id=(level * PLANE_KA + to // band_size, lax.rem(to, band_size)),
                device_id_type=MESH,
            ).start()

    def prepare(q):
        wait_bytes(g3_recv.at[q, pl.ds(0, plane_size - 1)], recv_sem.at[7 + q])

        @pl.loop(0, plane_size)
        def _(c):
            tri_f[pl.ds(pl.multiple_of(c * 40, 8), 40), :] = g3_recv[q, c].astype(F32)

        for n, (i, j) in enumerate(blocks):
            block = tri_f[n * 128 : (n + 1) * 128, :]
            screen[i * 128 : (i + 1) * 128, j * 128 : (j + 1) * 128] = block.astype(BF16)
            if i != j:
                screen[j * 128 : (j + 1) * 128, i * 128 : (i + 1) * 128] = block.T.astype(BF16)
        screened[...] = dot(coeffs[q], screen[...]).astype(BF16)

    def respond(q):
        step = field_a.shape[1]
        per = quarter // step

        def locate(n):
            part = lax.rem(band + 1 + n // per, band_size)
            inner = pl.multiple_of(lax.rem(n, per) * step, 128)
            cols = pl.ds(pl.multiple_of(part * quarter + inner, 128), step)
            return part, pl.ds(inner, step), cols

        def expand(n, field):
            field[...] = dot(screened[...], basis[:, locate(n)[2]])

        def contract(n, field):
            part, inner, cols = locate(n)
            for k in range(2):
                near = virt_f[k, :, cols]
                total = jnp.zeros((32, step), F32)
                lines = []
                for i in range(8):
                    first = k * 256 + i * 32
                    piece = field[first : first + 32, :]
                    total += piece * occ_f[q, part, k * 8 + i : k * 8 + i + 1, inner]
                    lines.append(jnp.sum(piece * near, axis=0, keepdims=True))
                lines = jnp.concatenate(lines, axis=0)
                cb_send[q, part, k * 8 : (k + 1) * 8, inner] = lines.astype(BF16)
                rounded = total.astype(BF16).astype(F32)
                if q == 0:
                    virt_acc[k, :, cols] = rounded
                else:
                    virt_out[k, :, cols] = (virt_acc[k, :, cols] + rounded).astype(BF16)

        expand(0, field_a)
        for j in range(band_size):

            @pl.loop(0, per // 2)
            def _(t):
                n = j * per + 2 * t
                expand(n + 1, field_b)
                contract(n, field_a)
                expand(lax.rem(n + 2, per * band_size), field_a)
                contract(n + 1, field_b)

            to = lax.rem(band + 1 + j, band_size)
            if j < band_size - 1:
                pltpu.make_async_remote_copy(
                    src_ref=cb_send.at[q, to],
                    dst_ref=cb_recv.at[q, band],
                    send_sem=send_sem.at[9 + 3 * q],
                    recv_sem=recv_sem.at[9 + 3 * q],
                    device_id=(ka, to),
                    device_id_type=MESH,
                ).start()
            else:
                cb_recv[q, band] = cb_send[q, band]

    begin()
    project(0)
    project(1)
    exchange(0)
    exchange(1)
    collect(0)
    collect(1)
    prepare(0)
    respond(0)
    prepare(1)
    respond(1)

    row, col = iota((256, 128), 0), iota((256, 128), 1)
    sent = jnp.zeros((256, 128), F32)
    for q in range(2):
        split_c = ones_where(
            ((row & 3) == 2 * q + ((col >> 3) & 1)) & ((row >> 5) == (col & 7)) & (((row >> 2) & 7) == (col >> 4))
        )
        wait_bytes(cb_recv.at[q, pl.ds(0, band_size - 1)], recv_sem.at[9 + 3 * q])
        total = jnp.sum(cb_recv[q].astype(F32), axis=0)
        tall = jnp.concatenate([total[:, c * 128 : (c + 1) * 128] for c in range(chunks)], axis=0)
        sent += dot(split_c, tall.astype(BF16))
    c1_send[...] = sent.reshape(64, 4, 128).astype(BF16)
    row, col = iota((128, 128), 0), iota((128, 128), 1)
    fold_c = ones_where(
        ((col & 1) == ((row >> 3) & 1)) & ((col >> 4) == (row & 7)) & (((col >> 1) & 7) == (row >> 4))
    )
    spread(c1_send, c1_recv, 10)
    wait_bytes(c1_recv.at[pl.ds(0, ka_size - 1)], recv_sem.at[10])
    got = c1_recv[...].astype(F32).reshape(256, 128).astype(BF16)
    c2_send[...] = (dot(pick_c[...], got) * occ_scale).reshape(64, 2, 128).astype(BF16)
    spread(c2_send, c2_recv, 11)
    wait_bytes(c2_recv.at[pl.ds(0, ka_size - 1)], recv_sem.at[11])
    got = c2_recv[...].astype(F32).reshape(128, 128).astype(BF16)
    folded = dot(fold_c, got)
    for c in range(chunks):
        for k in range(2):
            first = c * 16 + k * 8
            occ_out[k, :, c * 128 : (c + 1) * 128] = folded[first : first + 8].astype(BF16)

    for index, buffer in ((0, a1_recv), (1, a2_recv), (10, c1_recv), (11, c2_recv)):
        wait_bytes(buffer.at[pl.ds(0, ka_size - 1)], send_sem.at[index])
    wait_bytes(en_all.at[pl.ds(0, ka_size - 1)], send_sem.at[2])
    for q in range(2):
        wait_bytes(cb_recv.at[q, pl.ds(0, band_size - 1)], send_sem.at[9 + 3 * q])
        wait_bytes(occ_b.at[q, pl.ds(0, band_size - 1)], send_sem.at[13 + q])
        wait_bytes(g1_recv.at[q, pl.ds(0, plane_size - 1)], send_sem.at[3 + q])
        wait_bytes(g2_recv.at[q, pl.ds(0, depth - 1)], send_sem.at[5 + q])
        wait_bytes(g3_recv.at[q, pl.ds(0, plane_size - 1)], send_sem.at[7 + q])


def shards(occupied, virtual, occ_energy, virt_energy, partner, coulomb, basis):
    local_k, occ_count, grid_count = occupied.shape
    group_count = virtual.shape[1]
    aux_count = basis.shape[0]
    transfers = partner.shape[0]
    ka_size = lax.axis_size("ka")
    band_size = lax.axis_size("band")
    total_k = local_k * ka_size
    virt_count = group_count * band_size
    quarter = grid_count // band_size
    gram_scale = 1.0 / math.sqrt(total_k * occ_count * virt_count * aux_count)
    occ_scale = 1.0 / math.sqrt(transfers * virt_count)
    plane = PLANE_KA * band_size
    depth = ka_size // PLANE_KA
    hop_2 = pltpu.VMEM((ka_size, 2, 128), BF16)
    hop_4 = pltpu.VMEM((ka_size, 4, 128), BF16)
    virt_energy = virt_energy.T
    vmem = pl.BlockSpec(memory_space=pltpu.VMEM)
    hbm = pl.BlockSpec(memory_space=pl.ANY)
    scratch = dict(
        occ=pltpu.VMEM(occupied.shape, BF16),
        virt=pltpu.VMEM(virtual.shape, BF16),
        occ_en=pltpu.VMEM(occ_energy.shape, F32),
        virt_en=pltpu.VMEM(virt_energy.shape, F32),
        partner=pltpu.VMEM(partner.shape, jnp.int32),
        coul=pltpu.VMEM(coulomb.shape, F32),
        basis=pltpu.VMEM(basis.shape, BF16),
        virt_f=pltpu.VMEM(virtual.shape, F32),
        en_s=pltpu.VMEM((2, 128), F32),
        en_all=pltpu.VMEM((ka_size, 2, 128), F32),
        a1_send=hop_2,
        a1_recv=hop_2,
        a2_send=hop_4,
        a2_recv=hop_4,
        occ_b=pltpu.VMEM((2, band_size, 16, quarter), BF16),
        occ_f=pltpu.VMEM((2, band_size, 16, quarter), F32),
        pick_a=pltpu.VMEM((256, 128), BF16),
        pick_c=pltpu.VMEM((128, 256), BF16),
        scale_s=pltpu.VMEM((2, 1280, 128), F32),
        coeffs=pltpu.VMEM((2, 512, aux_count), BF16),
        pairs_a=pltpu.VMEM((512, quarter), BF16),
        pairs_b=pltpu.VMEM((512, quarter), BF16),
        acc=pltpu.VMEM((2, 512, aux_count), F32),
        weighted=pltpu.VMEM((512, aux_count), BF16),
        tri_f=pltpu.VMEM((1280, 128), F32),
        g1_send=pltpu.VMEM((2, plane, 40, 128), BF16),
        g1_recv=pltpu.VMEM((2, plane, 40, 128), BF16),
        g2_send=pltpu.VMEM((2, 40, 128), BF16),
        g2_recv=pltpu.VMEM((2, depth, 40, 128), BF16),
        g3_recv=pltpu.VMEM((2, plane, 40, 128), BF16),
        screen=pltpu.VMEM((aux_count, aux_count), BF16),
        screened=pltpu.VMEM((512, aux_count), BF16),
        field_a=pltpu.VMEM((512, 512), F32),
        field_b=pltpu.VMEM((512, 512), F32),
        virt_acc=pltpu.VMEM(virtual.shape, F32),
        cb_send=pltpu.VMEM((2, band_size, 16, quarter), BF16),
        cb_recv=pltpu.VMEM((2, band_size, 16, quarter), BF16),
        c1_send=hop_4,
        c1_recv=hop_4,
        c2_send=hop_2,
        c2_recv=hop_2,
        table=pltpu.SMEM(partner.shape, jnp.int32),
        load_sem=pltpu.SemaphoreType.DMA((8,)),
        send_sem=pltpu.SemaphoreType.DMA((15,)),
        recv_sem=pltpu.SemaphoreType.DMA((19,)),
    )
    return pl.pallas_call(
        functools.partial(kernel, ka_size, band_size, gram_scale, occ_scale),
        out_shape=(
            jax.ShapeDtypeStruct((local_k, occ_count, quarter), BF16),
            jax.ShapeDtypeStruct(virtual.shape, BF16),
        ),
        in_specs=[hbm] * 7,
        out_specs=(vmem, vmem),
        scratch_shapes=list(scratch.values()),
        compiler_params=pltpu.CompilerParams(
            collective_id=0, has_side_effects=True, vmem_limit_bytes=60 * 1024 * 1024
        ),
    )(occupied, virtual, occ_energy, virt_energy, partner, coulomb, basis)


def solution(mesh):
    in_specs = (
        P("ka", None, None),
        P("ka", "band", None),
        P("ka", None),
        P(None, "band"),
        P(),
        P(),
        P(),
    )
    out_specs = (P("ka", None, "band"), P("ka", "band", None))
    return jax.shard_map(shards, mesh=mesh, in_specs=in_specs, out_specs=out_specs, check_vma=False)
```

```python
import functools
import math

import jax
import jax.numpy as jnp
from jax import lax
from jax.experimental import pallas as pl
from jax.experimental.pallas import tpu as pltpu
from jax.sharding import PartitionSpec as P

FREQUENCY = 2.5
BROADENING = 0.4
F32 = jnp.float32
BF16 = jnp.bfloat16
MESH = pl.DeviceIdType.MESH
PLANE_KA = 8


def response(energy_gaps):
    shifted = FREQUENCY - energy_gaps
    return shifted / (shifted * shifted + BROADENING * BROADENING)


def dot(left, right):
    return lax.dot_general(left, right, (((1,), (0,)), ((), ())), preferred_element_type=F32)


def dot_t(left, right):
    return lax.dot_general(left, right, (((1,), (1,)), ((), ())), preferred_element_type=F32)


def dot_rows(left, right):
    return lax.dot_general(left, right, (((0,), (0,)), ((), ())), preferred_element_type=F32)


def iota(shape, axis):
    return lax.broadcasted_iota(jnp.int32, shape, axis)


def ones_where(mask):
    return jnp.where(mask, 1.0, 0.0).astype(BF16)


def wait_bytes(ref, sem):
    pltpu.make_async_copy(ref, ref, sem).wait()


def kernel(
    ka_size, band_size, gram_scale, occ_scale,
    occ_hbm, virt_hbm, occ_en_hbm, virt_en_hbm, partner_hbm, coul_hbm, basis_hbm,
    occ_out, virt_hbm_out,
    occ_ref, virt, occ_en_ref, virt_en_ref, partner_ref, coul_ref, basis, virt_f, en_s, en_all,
    a1_send, a1_recv, a2_send, a2_recv, occ_b, occ_f, pick_a, pick_c, scale_s, coeffs, pairs_a, pairs_b,
    acc, weighted, tri_f, g1_send, g1_recv, g2_send, g2_recv, g3_recv, screen, screened,
    field_a, field_b, virt_acc, virt_out, cb_send, cb_recv, c1_send, c1_recv, c2_send, c2_recv, table,
    load_sem, send_sem, recv_sem,
):
    ka = lax.axis_index("ka")
    band = lax.axis_index("band")
    plane_size = PLANE_KA * band_size
    depth = ka_size // PLANE_KA
    place = lax.rem(ka, PLANE_KA) * band_size + band
    level = ka // PLANE_KA
    quarter = occ_hbm.shape[2] // band_size
    chunks = quarter // 128

    loaded = (
        (occ_hbm, occ_ref), (occ_en_hbm, occ_en_ref), (partner_hbm, partner_ref), (coul_hbm, coul_ref),
        (virt_en_hbm, virt_en_ref), (partner_hbm, table), (virt_hbm, virt), (basis_hbm, basis),
    )
    loads = [pltpu.make_async_copy(a, b, load_sem.at[n]) for n, (a, b) in enumerate(loaded)]
    for load in loads:
        load.start()

    barrier = pltpu.get_barrier_semaphore()

    @pl.loop(1, ka_size)
    def _(off):
        to = (lax.rem(ka + off, ka_size), band)
        pl.semaphore_signal(barrier, inc=1, device_id=to, device_id_type=MESH)

    for band_off in range(1, band_size):
        near = lax.rem(band + band_off, band_size)

        @pl.loop(0, PLANE_KA)
        def _(off):
            to = (level * PLANE_KA + lax.rem(ka + off, PLANE_KA), near)
            pl.semaphore_signal(barrier, inc=1, device_id=to, device_id_type=MESH)

    load_occ, load_occ_en, load_partner, load_coul, load_virt_en, load_table, load_virt, load_basis = loads

    def spread(source, target, index):
        @pl.loop(1, ka_size)
        def _(off):
            to = lax.rem(ka + off, ka_size)
            pltpu.make_async_remote_copy(
                src_ref=source.at[to],
                dst_ref=target.at[ka],
                send_sem=send_sem.at[index],
                recv_sem=recv_sem.at[index],
                device_id=(to, band),
                device_id_type=MESH,
            ).start()

        target[ka] = source[ka]

    row, col = iota((128, 128), 0), iota((128, 128), 1)
    slice_of, k_of = row >> 1, row & 1
    split_a = ones_where(
        ((slice_of >> 3) == (col & 7)) & ((slice_of & 7) == (col >> 4)) & (((col >> 3) & 1) == k_of)
    )
    load_occ.wait()
    tiles = []
    for c in range(chunks):
        cols = pl.ds(pl.multiple_of(band * quarter + c * 128, 128), 128)
        tiles += [occ_ref[0, :, cols].astype(F32), occ_ref[1, :, cols].astype(F32)]
    tall = jnp.concatenate(tiles, axis=0).astype(BF16)
    a1_send[...] = dot(split_a, tall).reshape(64, 2, 128).astype(BF16)
    load_occ_en.wait()
    en_s[...] = jnp.zeros_like(en_s)
    en_s[:, 0:8] = occ_en_ref[...]
    pl.semaphore_wait(barrier, ka_size - 1 + (band_size - 1) * PLANE_KA)
    spread(a1_send, a1_recv, 0)

    @pl.loop(1, ka_size)
    def _(off):
        pltpu.make_async_remote_copy(
            src_ref=en_s,
            dst_ref=en_all.at[ka],
            send_sem=send_sem.at[2],
            recv_sem=recv_sem.at[2],
            device_id=(lax.rem(ka + off, ka_size), band),
            device_id_type=MESH,
        ).start()

    en_all[ka] = en_s[...]

    load_partner.wait()
    row, col = iota((256, 128), 0), iota((256, 128), 1)
    own_k = 2 * (row >> 2) + (row & 1)
    table_a = jnp.where(((row >> 1) & 1) == 0, partner_ref[0:1, :].astype(F32), partner_ref[1:2, :].astype(F32))
    source = jnp.sum(jnp.where(col == own_k, table_a, 0.0), axis=1, keepdims=True)
    pick_a[...] = ones_where(col == source.astype(jnp.int32))
    row, col = iota((128, 128), 0), iota((128, 128), 1)
    wide_col = iota((128, 256), 1)
    moved_c = jnp.zeros((128, 256), F32)
    for q in range(2):
        chosen = jnp.where(row == col, partner_ref[q : q + 1, :].astype(F32), 0.0)
        source = jnp.sum(chosen, axis=1, keepdims=True).astype(jnp.int32)
        moved_c += jnp.where(wide_col == (source >> 1) * 4 + 2 * q + (source & 1), 1.0, 0.0)
    pick_c[...] = moved_c.astype(BF16)
    row, col = iota((256, 256), 0), iota((256, 256), 1)
    fold_a = ones_where(
        ((col & 3) == ((row >> 3) & 3)) & ((col >> 5) == (row & 7)) & (((col >> 2) & 7) == (row >> 5))
    )

    load_coul.wait()
    blocks = [(i, j) for i in range(4) for j in range(i, 4)]
    for q in range(2):
        rows_b, cols_b = [], []
        for i in range(4):
            line = coul_ref[q : q + 1, i * 128 : (i + 1) * 128]
            full = jnp.broadcast_to(line, (128, 128))
            cols_b.append(full)
            rows_b.append(full.T)
        for n, (i, j) in enumerate(blocks):
            scale_s[q, n * 128 : (n + 1) * 128, :] = rows_b[i] * cols_b[j] * gram_scale

    load_virt_en.wait()
    virt_cols = []
    for k in range(2):
        full = jnp.where(iota((32, 128), 1) == 2 * ka + k, virt_en_ref[...], 0.0)
        virt_cols.append(jnp.broadcast_to(jnp.sum(full, axis=1, keepdims=True), (32, 128)))

    load_virt.wait()
    virt_f[...] = virt[...].astype(F32)

    wait_bytes(a1_recv.at[pl.ds(0, ka_size - 1)], recv_sem.at[0])
    got = a1_recv[...].astype(F32).reshape(128, 128).astype(BF16)
    a2_send[...] = dot(pick_a[...], got).reshape(64, 4, 128).astype(BF16)
    spread(a2_send, a2_recv, 1)
    load_basis.wait()
    load_table.wait()
    wait_bytes(en_all.at[pl.ds(0, ka_size - 1)], recv_sem.at[2])
    energies = []
    for q in range(2):
        for k in range(2):
            other = table[q, 2 * ka + k]
            energies.append(en_all[other // 2, pl.ds(lax.rem(other, 2), 1), :])
    wait_bytes(a2_recv.at[pl.ds(0, ka_size - 1)], recv_sem.at[1])
    got = a2_recv[...].astype(F32).reshape(256, 128).astype(BF16)
    folded = dot(fold_a, got)
    for q in range(2):
        for c in range(chunks):
            tile = folded[c * 32 + q * 16 : c * 32 + (q + 1) * 16]
            cols = slice(c * 128, (c + 1) * 128)
            occ_b[q, band, :, cols] = tile.astype(BF16)
            occ_f[q, band, :, cols] = tile

    for q in range(2):
        for off in range(1, band_size):
            to = lax.rem(band + band_size - off, band_size)
            pltpu.make_async_remote_copy(
                src_ref=occ_b.at[q, band],
                dst_ref=occ_b.at[q, band],
                send_sem=send_sem.at[13 + q],
                recv_sem=recv_sem.at[13 + 3 * q + off - 1],
                device_id=(ka, to),
                device_id_type=MESH,
            ).start()

    def build(q, b, pairs):
        part = lax.rem(band + b, band_size)
        cols = pl.ds(pl.multiple_of(part * quarter, 128), quarter)
        for k in range(2):
            for i in range(8):
                n = k * 8 + i
                line = jnp.broadcast_to(occ_f[q, part, n : n + 1, :], (16, quarter)).astype(BF16)
                first = k * 256 + i * 32
                pairs[first : first + 16, :] = virt[k, 0:16, cols] * line
                pairs[first + 16 : first + 32, :] = virt[k, 16:32, cols] * line
        return cols

    def begin():
        cols = build(0, 0, pairs_a)
        build(1, 0, pairs_b)
        acc[0] = dot_t(pairs_a[...], basis[:, cols])
        acc[1] = dot_t(pairs_b[...], basis[:, cols])

    def project(q):
        for b in range(1, band_size):
            part = lax.rem(band + b, band_size)
            wait_bytes(occ_b.at[q, part], recv_sem.at[13 + 3 * q + b - 1])
            occ_f[q, part] = occ_b[q, part].astype(F32)
        buffers = (pairs_a, pairs_b)
        cols = build(q, 1, buffers[1])
        for b in range(1, band_size):
            now = cols
            if b + 1 < band_size:
                cols = build(q, b + 1, buffers[(b + 1) % 2])
            acc[q] += dot_t(buffers[b % 2][...], basis[:, now])
        coeffs[q] = acc[q].astype(BF16)
        for k in range(2):
            for i in range(8):
                energy = jnp.broadcast_to(energies[2 * q + k][:, i : i + 1], (32, 128))
                weight = response(virt_cols[k] - energy)
                rows = slice(k * 256 + i * 32, k * 256 + (i + 1) * 32)
                for j in range(4):
                    cols = slice(j * 128, (j + 1) * 128)
                    weighted[rows, cols] = (coeffs[q, rows, cols].astype(F32) * weight).astype(BF16)
        n = 0
        for i in range(4):
            part = dot_rows(weighted[:, i * 128 : (i + 1) * 128], coeffs[q, :, i * 128 :])
            for j in range(4 - i):
                tri_f[n * 128 : (n + 1) * 128, :] = part[:, j * 128 : (j + 1) * 128]
                n += 1

        @pl.loop(0, plane_size)
        def _(c):
            g1_send[q, c] = tri_f[pl.ds(pl.multiple_of(c * 40, 8), 40), :].astype(BF16)

        @pl.loop(1, plane_size)
        def _(off):
            to = lax.rem(place + off, plane_size)
            pltpu.make_async_remote_copy(
                src_ref=g1_send.at[q, to],
                dst_ref=g1_recv.at[q, place],
                send_sem=send_sem.at[3 + q],
                recv_sem=recv_sem.at[3 + q],
                device_id=(level * PLANE_KA + to // band_size, lax.rem(to, band_size)),
                device_id_type=MESH,
            ).start()

        g1_recv[q, place] = g1_send[q, place]

    def exchange(q):
        wait_bytes(g1_recv.at[q, pl.ds(0, plane_size - 1)], recv_sem.at[3 + q])
        total = jnp.sum(g1_recv[q].astype(F32), axis=0).astype(BF16)
        g2_send[q] = total
        g2_recv[q, level] = total

        @pl.loop(1, depth)
        def _(off):
            to = lax.rem(level + off, depth)
            pltpu.make_async_remote_copy(
                src_ref=g2_send.at[q],
                dst_ref=g2_recv.at[q, level],
                send_sem=send_sem.at[5 + q],
                recv_sem=recv_sem.at[5 + q],
                device_id=(to * PLANE_KA + lax.rem(ka, PLANE_KA), band),
                device_id_type=MESH,
            ).start()

    def collect(q):
        wait_bytes(g2_recv.at[q, pl.ds(0, depth - 1)], recv_sem.at[5 + q])
        total = jnp.sum(g2_recv[q].astype(F32), axis=0)
        scale = scale_s[q, pl.ds(pl.multiple_of(place * 40, 8), 40), :]
        g3_recv[q, place] = (total * scale).astype(BF16)

        @pl.loop(1, plane_size)
        def _(off):
            to = lax.rem(place + off, plane_size)
            pltpu.make_async_remote_copy(
                src_ref=g3_recv.at[q, place],
                dst_ref=g3_recv.at[q, place],
                send_sem=send_sem.at[7 + q],
                recv_sem=recv_sem.at[7 + q],
                device_id=(level * PLANE_KA + to // band_size, lax.rem(to, band_size)),
                device_id_type=MESH,
            ).start()

    def prepare(q):
        wait_bytes(g3_recv.at[q, pl.ds(0, plane_size - 1)], recv_sem.at[7 + q])

        @pl.loop(0, plane_size)
        def _(c):
            tri_f[pl.ds(pl.multiple_of(c * 40, 8), 40), :] = g3_recv[q, c].astype(F32)

        for n, (i, j) in enumerate(blocks):
            block = tri_f[n * 128 : (n + 1) * 128, :]
            screen[i * 128 : (i + 1) * 128, j * 128 : (j + 1) * 128] = block.astype(BF16)
            if i != j:
                screen[j * 128 : (j + 1) * 128, i * 128 : (i + 1) * 128] = block.T.astype(BF16)
        screened[...] = dot(coeffs[q], screen[...]).astype(BF16)

    def respond(q):
        step = field_a.shape[1]
        per = quarter // step

        def locate(n):
            part = lax.rem(band + 1 + n // per, band_size)
            inner = pl.multiple_of(lax.rem(n, per) * step, 128)
            cols = pl.ds(pl.multiple_of(part * quarter + inner, 128), step)
            return part, pl.ds(inner, step), cols

        def expand(n, field):
            field[...] = dot(screened[...], basis[:, locate(n)[2]])

        def contract(n, field):
            part, inner, cols = locate(n)
            for k in range(2):
                near = virt_f[k, :, cols]
                total = jnp.zeros((32, step), F32)
                lines = []
                for i in range(8):
                    first = k * 256 + i * 32
                    piece = field[first : first + 32, :]
                    total += piece * occ_f[q, part, k * 8 + i : k * 8 + i + 1, inner]
                    lines.append(jnp.sum(piece * near, axis=0, keepdims=True))
                lines = jnp.concatenate(lines, axis=0)
                cb_send[q, part, k * 8 : (k + 1) * 8, inner] = lines.astype(BF16)
                rounded = total.astype(BF16).astype(F32)
                if q == 0:
                    virt_acc[k, :, cols] = rounded
                else:
                    virt_out[k, :, cols] = (virt_acc[k, :, cols] + rounded).astype(BF16)

        expand(0, field_a)
        for j in range(band_size):

            @pl.loop(0, per // 2)
            def _(t):
                n = j * per + 2 * t
                expand(n + 1, field_b)
                contract(n, field_a)
                expand(lax.rem(n + 2, per * band_size), field_a)
                contract(n + 1, field_b)

            to = lax.rem(band + 1 + j, band_size)
            if j < band_size - 1:
                pltpu.make_async_remote_copy(
                    src_ref=cb_send.at[q, to],
                    dst_ref=cb_recv.at[q, band],
                    send_sem=send_sem.at[9 + 3 * q],
                    recv_sem=recv_sem.at[9 + 3 * q],
                    device_id=(ka, to),
                    device_id_type=MESH,
                ).start()
            else:
                cb_recv[q, band] = cb_send[q, band]

    begin()
    project(0)
    project(1)
    exchange(0)
    exchange(1)
    collect(0)
    collect(1)
    prepare(0)
    respond(0)
    prepare(1)
    respond(1)

    store_virt = pltpu.make_async_copy(virt_out, virt_hbm_out, load_sem.at[8])
    store_virt.start()

    row, col = iota((256, 128), 0), iota((256, 128), 1)
    sent = jnp.zeros((256, 128), F32)
    for q in range(2):
        split_c = ones_where(
            ((row & 3) == 2 * q + ((col >> 3) & 1)) & ((row >> 5) == (col & 7)) & (((row >> 2) & 7) == (col >> 4))
        )
        wait_bytes(cb_recv.at[q, pl.ds(0, band_size - 1)], recv_sem.at[9 + 3 * q])
        total = jnp.sum(cb_recv[q].astype(F32), axis=0)
        tall = jnp.concatenate([total[:, c * 128 : (c + 1) * 128] for c in range(chunks)], axis=0)
        sent += dot(split_c, tall.astype(BF16))
    c1_send[...] = sent.reshape(64, 4, 128).astype(BF16)
    row, col = iota((128, 128), 0), iota((128, 128), 1)
    fold_c = ones_where(
        ((col & 1) == ((row >> 3) & 1)) & ((col >> 4) == (row & 7)) & (((col >> 1) & 7) == (row >> 4))
    )
    spread(c1_send, c1_recv, 10)
    wait_bytes(c1_recv.at[pl.ds(0, ka_size - 1)], recv_sem.at[10])
    got = c1_recv[...].astype(F32).reshape(256, 128).astype(BF16)
    c2_send[...] = (dot(pick_c[...], got) * occ_scale).reshape(64, 2, 128).astype(BF16)
    spread(c2_send, c2_recv, 11)
    wait_bytes(c2_recv.at[pl.ds(0, ka_size - 1)], recv_sem.at[11])
    got = c2_recv[...].astype(F32).reshape(128, 128).astype(BF16)
    folded = dot(fold_c, got)
    for c in range(chunks):
        for k in range(2):
            first = c * 16 + k * 8
            occ_out[k, :, c * 128 : (c + 1) * 128] = folded[first : first + 8].astype(BF16)

    store_virt.wait()

    for index, buffer in ((0, a1_recv), (1, a2_recv), (10, c1_recv), (11, c2_recv)):
        wait_bytes(buffer.at[pl.ds(0, ka_size - 1)], send_sem.at[index])
    wait_bytes(en_all.at[pl.ds(0, ka_size - 1)], send_sem.at[2])
    for q in range(2):
        wait_bytes(cb_recv.at[q, pl.ds(0, band_size - 1)], send_sem.at[9 + 3 * q])
        wait_bytes(occ_b.at[q, pl.ds(0, band_size - 1)], send_sem.at[13 + q])
        wait_bytes(g1_recv.at[q, pl.ds(0, plane_size - 1)], send_sem.at[3 + q])
        wait_bytes(g2_recv.at[q, pl.ds(0, depth - 1)], send_sem.at[5 + q])
        wait_bytes(g3_recv.at[q, pl.ds(0, plane_size - 1)], send_sem.at[7 + q])


def shards(occupied, virtual, occ_energy, virt_energy, partner, coulomb, basis):
    local_k, occ_count, grid_count = occupied.shape
    group_count = virtual.shape[1]
    aux_count = basis.shape[0]
    transfers = partner.shape[0]
    ka_size = lax.axis_size("ka")
    band_size = lax.axis_size("band")
    total_k = local_k * ka_size
    virt_count = group_count * band_size
    quarter = grid_count // band_size
    gram_scale = 1.0 / math.sqrt(total_k * occ_count * virt_count * aux_count)
    occ_scale = 1.0 / math.sqrt(transfers * virt_count)
    plane = PLANE_KA * band_size
    depth = ka_size // PLANE_KA
    hop_2 = pltpu.VMEM((ka_size, 2, 128), BF16)
    hop_4 = pltpu.VMEM((ka_size, 4, 128), BF16)
    virt_energy = virt_energy.T
    vmem = pl.BlockSpec(memory_space=pltpu.VMEM)
    hbm = pl.BlockSpec(memory_space=pl.ANY)
    scratch = dict(
        occ=pltpu.VMEM(occupied.shape, BF16),
        virt=pltpu.VMEM(virtual.shape, BF16),
        occ_en=pltpu.VMEM(occ_energy.shape, F32),
        virt_en=pltpu.VMEM(virt_energy.shape, F32),
        partner=pltpu.VMEM(partner.shape, jnp.int32),
        coul=pltpu.VMEM(coulomb.shape, F32),
        basis=pltpu.VMEM(basis.shape, BF16),
        virt_f=pltpu.VMEM(virtual.shape, F32),
        en_s=pltpu.VMEM((2, 128), F32),
        en_all=pltpu.VMEM((ka_size, 2, 128), F32),
        a1_send=hop_2,
        a1_recv=hop_2,
        a2_send=hop_4,
        a2_recv=hop_4,
        occ_b=pltpu.VMEM((2, band_size, 16, quarter), BF16),
        occ_f=pltpu.VMEM((2, band_size, 16, quarter), F32),
        pick_a=pltpu.VMEM((256, 128), BF16),
        pick_c=pltpu.VMEM((128, 256), BF16),
        scale_s=pltpu.VMEM((2, 1280, 128), F32),
        coeffs=pltpu.VMEM((2, 512, aux_count), BF16),
        pairs_a=pltpu.VMEM((512, quarter), BF16),
        pairs_b=pltpu.VMEM((512, quarter), BF16),
        acc=pltpu.VMEM((2, 512, aux_count), F32),
        weighted=pltpu.VMEM((512, aux_count), BF16),
        tri_f=pltpu.VMEM((1280, 128), F32),
        g1_send=pltpu.VMEM((2, plane, 40, 128), BF16),
        g1_recv=pltpu.VMEM((2, plane, 40, 128), BF16),
        g2_send=pltpu.VMEM((2, 40, 128), BF16),
        g2_recv=pltpu.VMEM((2, depth, 40, 128), BF16),
        g3_recv=pltpu.VMEM((2, plane, 40, 128), BF16),
        screen=pltpu.VMEM((aux_count, aux_count), BF16),
        screened=pltpu.VMEM((512, aux_count), BF16),
        field_a=pltpu.VMEM((512, 512), F32),
        field_b=pltpu.VMEM((512, 512), F32),
        virt_acc=pltpu.VMEM(virtual.shape, F32),
        virt_out=pltpu.VMEM(virtual.shape, BF16),
        cb_send=pltpu.VMEM((2, band_size, 16, quarter), BF16),
        cb_recv=pltpu.VMEM((2, band_size, 16, quarter), BF16),
        c1_send=hop_4,
        c1_recv=hop_4,
        c2_send=hop_2,
        c2_recv=hop_2,
        table=pltpu.SMEM(partner.shape, jnp.int32),
        load_sem=pltpu.SemaphoreType.DMA((9,)),
        send_sem=pltpu.SemaphoreType.DMA((15,)),
        recv_sem=pltpu.SemaphoreType.DMA((19,)),
    )
    return pl.pallas_call(
        functools.partial(kernel, ka_size, band_size, gram_scale, occ_scale),
        out_shape=(
            jax.ShapeDtypeStruct((local_k, occ_count, quarter), BF16),
            jax.ShapeDtypeStruct(virtual.shape, BF16),
        ),
        in_specs=[hbm] * 7,
        out_specs=(vmem, hbm),
        scratch_shapes=list(scratch.values()),
        compiler_params=pltpu.CompilerParams(
            collective_id=0, has_side_effects=True, vmem_limit_bytes=60 * 1024 * 1024
        ),
    )(occupied, virtual, occ_energy, virt_energy, partner, coulomb, basis)


def solution(mesh):
    in_specs = (
        P("ka", None, None),
        P("ka", "band", None),
        P("ka", None),
        P(None, "band"),
        P(),
        P(),
        P(),
    )
    out_specs = (P("ka", None, "band"), P("ka", "band", None))
    return jax.shard_map(shards, mesh=mesh, in_specs=in_specs, out_specs=out_specs, check_vma=False)
```
